256 devices in a mesh: grp: 2 (over core), smp: 8 (over x_lo, y), seq: 16 (over x_hi, z).
Axes of the slice: x: 4 (x_hi: 2, x_lo: 2; x = x_hi * 2 + x_lo), y: 4, z: 8, core: 2. Of those that a mesh axis runs over, the one named last changes fastest.
Arguments:
- resp_q: bfloat16 [16, 2048, 4096], P(('grp', 'smp'), 'seq'), parts along dimension 0, may hold values from -6.5 to 6.5
- resp_kv: bfloat16 [16, 2048, 1024], P(('grp', 'smp'), 'seq'), parts along dimension 0, may hold values from -8 to 8
- prompt_kv: bfloat16 [4096, 1024], P(('grp', 'smp', 'seq')), parts along dimension 0, may hold values from -8 to 8
- resp_len: int32 [16], P(('grp', 'smp')), parts along dimension 0, may hold values from 512 to 2048, as said below
- block_order: int32 [64], P('grp'), parts along dimension 0, may hold values from 0 to 31, each once
- tags: int32 [16, 32], P(('grp', 'smp'), 'seq'), parts along dimension 0, may hold values from 0 to 3
- ver_weight: float32 [4], replicated, may hold values from 0.25 to 2.5
Outputs:
- attended: bfloat16 [16, 2048, 4096], P(('grp', 'smp'), 'seq'), parts along dimension 0
The draws below stay inside these ranges and needn't reach their ends.
There are 2 independent parts, one for each index of `grp`. The reference program is written for one: setup_inputs(seed, part) draws one part's arguments, and reference() takes and returns one part's arrays. A program takes and returns all parts, laid end to end along the dimension named above; an argument that names none is the same for every part. Nothing has to cross between parts.
Inputs may be any that keep to these rules, and one draw needn't show every extreme that they name: `resp_len`: one response in every draw has all 2048 tokens live. `block_order`: each number once.
All inputs are finite; a program needn't handle non-finite values.
Results may differ from the reference program's by a relative error of at most 0.007.
Values may be sent and summed in bfloat16 or wider, within the bound.
A program may use at most 64 MiB of HBM per device.

```python
import math
import jax
import jax.numpy as jnp
from jax import lax

H = 32
KVH = 4
HD = 128
NVER = 4
SAMPLES = 8
RESP = 2048
PROMPT = 2048
BLK = 64
NBLK = 32


def pair_scales():
    column = jnp.arange(2 * KVH * HD)
    return jnp.where(column < KVH * HD, 2.0, 1.0).astype(jnp.float32)


def draw_resp_q(key, part):
    key = jax.random.fold_in(key, 1)
    base = jax.random.truncated_normal(key, -6.0, 6.0, (SAMPLES, RESP, H * HD), jnp.float32)
    return base.astype(jnp.bfloat16)


def draw_resp_kv(key, part):
    key = jax.random.fold_in(key, 2)
    scales = pair_scales()
    base = jax.random.truncated_normal(key, -4.0, 4.0, (SAMPLES, RESP, 2 * KVH * HD), jnp.float32)
    return (base * scales).astype(jnp.bfloat16)


def draw_prompt_kv(key, part):
    key = jax.random.fold_in(key, 3)
    scales = pair_scales()
    base = jax.random.truncated_normal(key, -4.0, 4.0, (PROMPT, 2 * KVH * HD), jnp.float32) * scales
    return base.astype(jnp.bfloat16)


def draw_resp_len(key, part):
    key = jax.random.fold_in(key, 4)
    lengths = jax.random.randint(key, (SAMPLES,), RESP // 4, RESP + 1)
    chosen = jax.random.randint(jax.random.fold_in(key, 5), (), 0, SAMPLES)
    return jnp.where(jnp.arange(SAMPLES) == chosen, RESP, lengths).astype(jnp.int32)


def plant(result, rng, least, top_value):
    longest = result.shape.index(max(result.shape))
    spots = []
    for shift in (0, 1):
        where = [jax.random.randint(jax.random.fold_in(rng, axis), (), 0, length) for axis, length in enumerate(result.shape)]
        where[longest] = (where[longest] + shift) % result.shape[longest]
        spots.append(tuple(where))
    return result.at[spots[0]].set(least).at[spots[1]].set(top_value)


def setup_inputs(seed: int = 0, part: int = 0) -> dict:
    key_of = jax.random.split(jax.random.key(seed), 8)
    part_keys = jax.random.split(jax.random.fold_in(key_of[7], part), 8)
    resp_q = draw_resp_q(jax.random.fold_in(jax.random.fold_in(key_of[7], part), 71), part)
    resp_kv = draw_resp_kv(jax.random.fold_in(jax.random.fold_in(key_of[7], part), 71), part)
    prompt_kv = draw_prompt_kv(jax.random.fold_in(jax.random.fold_in(key_of[7], part), 71), part)
    resp_len = draw_resp_len(jax.random.fold_in(jax.random.fold_in(key_of[7], part), 71), part)
    block_order = jax.random.permutation(part_keys[4], NBLK).astype(jnp.int32)
    tags = plant(jax.random.randint(part_keys[5], (SAMPLES, NBLK), 0, NVER), jax.random.fold_in(part_keys[5], 1), 0, NVER - 1).astype(jnp.int32)
    ver_weight = jnp.clip(jnp.exp(jax.random.uniform(key_of[6], (NVER,), jnp.float32, math.log(0.25), math.log(2.5))), 0.25, 2.5)
    return {"resp_q": resp_q, "resp_kv": resp_kv, "prompt_kv": prompt_kv, "resp_len": resp_len, "block_order": block_order, "tags": tags, "ver_weight": ver_weight}


masked_score = -1e30


def reference(resp_q, resp_kv, prompt_kv, resp_len, block_order, tags, ver_weight):
    group_width = H // KVH
    half_width = KVH * HD
    scaling = HD ** -0.5
    stored = jnp.arange(RESP, dtype=jnp.int32)
    positions = (block_order[stored // BLK] * BLK + stored % BLK).astype(jnp.int32)
    prompt_keys = prompt_kv[:, :half_width].astype(jnp.float32).reshape(PROMPT, KVH, HD)
    prompt_values = prompt_kv[:, half_width:].astype(jnp.float32).reshape(PROMPT, KVH, HD)
    prompt_live = jnp.ones((PROMPT,), dtype=bool)
    prompt_pos = jnp.full((PROMPT,), -1, dtype=jnp.int32)

    def one_response(inputs):
        queries, pairs, seq_length, tag_row = inputs
        keys = jnp.concatenate([prompt_keys, pairs[:, :half_width].astype(jnp.float32).reshape(RESP, KVH, HD)], 0)
        values = jnp.concatenate([prompt_values, pairs[:, half_width:].astype(jnp.float32).reshape(RESP, KVH, HD)], 0)
        key_live = jnp.concatenate([prompt_live, positions < seq_length])
        key_pos = jnp.concatenate([prompt_pos, positions])
        block_weight = jnp.take(ver_weight, tag_row)

        def one_block(block_inputs):
            block_q, block_pos, weight_now = block_inputs
            heads = block_q.astype(jnp.float32).reshape(BLK, KVH, group_width, HD)
            scores = jnp.einsum("qhgd,khd->hgqk", heads, keys, precision=lax.Precision.HIGHEST) * scaling
            allowed = key_live[None, :] & (key_pos[None, :] <= block_pos[:, None])
            scores = jnp.where(allowed, scores, masked_score)
            top = jnp.max(scores, axis=-1, keepdims=True)
            weights = jnp.where(allowed, jnp.exp(scores - top), 0.0)
            totals = jnp.sum(weights, axis=-1)
            rounded = lax.optimization_barrier(weights.astype(jnp.bfloat16)).astype(jnp.float32)
            mixed = jnp.einsum("hgqk,khd->qhgd", rounded, values, precision=lax.Precision.HIGHEST)
            mixed = mixed / totals.transpose(2, 0, 1)[..., None]
            row_weight = jnp.where(block_pos < seq_length, weight_now, 0.0)
            return (mixed.reshape(BLK, H * HD) * row_weight[:, None]).astype(jnp.bfloat16)

        outputs = lax.map(one_block, (queries.reshape(NBLK, BLK, H * HD), positions.reshape(NBLK, BLK), block_weight))
        return outputs.reshape(RESP, H * HD)

    return lax.map(one_response, (resp_q, resp_kv, resp_len, tags))
```

```python
import functools
import math

import jax
import jax.numpy as jnp
from jax import lax
from jax.experimental import pallas as pl
from jax.experimental.pallas import tpu as pltpu
from jax.sharding import PartitionSpec as P

MESH = pl.DeviceIdType.MESH
F32 = jnp.float32
BF16 = jnp.bfloat16
H = 32
KVH = 4
HD = 128
GW = H // KVH
HALF = KVH * HD
ROWS = 128
BLK = 64
NX, NY, NZ = 4, 4, 8
NPB = NX * NY
SCALE = HD**-0.5 * math.log2(math.e)
LEAST, MOST = 2.0**-80, 2.0**100

M_EXCH = 0
M_PIECE = 1
M_Z = M_PIECE + NZ - 1
M_X = M_Z + 16
M_Y = M_X + 4
N_MSG = M_Y + 16


def positions(order_ref, block, along, shape):
    index = lax.broadcasted_iota(jnp.int32, shape, along)
    first, second = order_ref[2 * block], order_ref[2 * block + 1]
    return jnp.where(index < BLK, first * BLK + index, second * BLK + index - BLK)


def row_scale(order_ref, len_ref, tags_ref, weight_ref, seq):
    shape = (1, ROWS)
    query_pos = positions(order_ref, seq, 1, shape)
    picked = []
    for k in range(2):
        value = jnp.float32(0.0)
        for v in range(weight_ref.shape[0]):
            value = jnp.where(tags_ref[0, k] == v, weight_ref[v], value)
        picked.append(value)
    index = lax.broadcasted_iota(jnp.int32, shape, 1)
    weight = jnp.where(index < BLK, picked[0], picked[1])
    return jnp.where(query_pos < len_ref[0], weight, 0.0)


def block_bias(order_ref, len_ref, seq, block):
    shape = (ROWS, ROWS)
    query_pos = positions(order_ref, seq, 1, shape)
    key_pos = positions(order_ref, block, 0, shape)
    allowed = (key_pos <= query_pos) & (key_pos < len_ref[0])
    return jnp.where(allowed, 0.0, -jnp.inf).astype(F32)


def gather_attend(
    len_ref, order_ref, tags_ref, weight_ref, q_ref, own_ref, piece_ref,
    out_ref, bad_ref, kept_ref,
    kv, qa, acc, bias, send_sem, recv_sem, keep_sem,
):
    grp, smp, seq = lax.axis_index("grp"), lax.axis_index("smp"), lax.axis_index("seq")
    x_hi, z = lax.div(seq, NZ), lax.rem(seq, NZ)
    x_lo, y = lax.div(smp, NY), lax.rem(smp, NY)
    x = x_hi * 2 + x_lo

    def device(dx, dy, dz):
        xx, yy, zz = lax.rem(x + dx + NX, NX), lax.rem(y + dy + NY, NY), lax.rem(z + dz + NZ, NZ)
        return (grp, lax.rem(xx, 2) * NY + yy, lax.div(xx, 2) * NZ + zz)

    def rblock(lane, dz):
        column = x_hi if lane == 0 else 1 - x_hi
        return NPB + column * NZ + lax.rem(z + dz + NZ, NZ)

    def pblock(dx, dy):
        return lax.rem(x + dx + NX, NX) * NY + lax.rem(y + dy + NY, NY)

    peers = [device(0, 0, d) for d in range(1, NZ)]
    peers += [device(d, 0, 0) for d in range(1, NX)] + [device(0, 1, 0), device(0, -1, 0)]
    barrier = pltpu.get_barrier_semaphore()
    for peer in peers:
        pl.semaphore_signal(barrier, inc=1, device_id=peer, device_id_type=MESH)

    def copy(message, src, dst, to):
        return pltpu.make_async_remote_copy(
            src_ref=src, dst_ref=dst, send_sem=send_sem.at[message], recv_sem=recv_sem.at[message],
            device_id=to, device_id_type=MESH,
        )

    parts = {"all": (0, ROWS), "low": (0, ROWS // 2), "high": (ROWS // 2, ROWS // 2)}
    started = {}

    def part_of(block, part):
        start, size = parts[part]
        return kv.at[block, pl.ds(start, size), :]

    def send(message, block, part, to, src=None):
        there = part_of(block, part)
        started[message] = part
        copy(message, there if src is None else src, there, to).start()

    def arrive(message, block, part="all"):
        here = part_of(block, part)
        copy(message, here, here, device(0, 0, 1)).wait_recv()

    for h in range(KVH):
        for g in range(GW):
            column = (h * GW + g) * HD
            scaled = q_ref[:, column : column + HD].T.astype(F32) * SCALE
            high = scaled.astype(BF16)
            qa[h, 0:HD, g * ROWS : (g + 1) * ROWS] = high
            qa[h, HD : 2 * HD, g * ROWS : (g + 1) * ROWS] = (scaled - high.astype(F32)).astype(BF16)
    own_block, own_prompt = rblock(0, 0), pblock(0, 0)
    kv[own_block] = own_ref[...]
    kv[own_prompt, pl.ds(pl.multiple_of(z * 16, 16), 16), :] = piece_ref[...]

    pl.semaphore_wait(barrier, len(peers))

    mine = kv.at[own_prompt, pl.ds(pl.multiple_of(z * 16, 16), 16), :]
    for d in (1, 7, 2, 6, 3, 5, 4):
        copy(M_PIECE + d - 1, piece_ref, mine, device(0, 0, d)).start()
    copy(M_EXCH, own_ref, kv.at[own_block], device(2, 0, 0)).start()
    started[M_EXCH] = "all"

    def z_step(lane, step):
        base = M_Z + lane * 8 + (step - 1) * 2
        low, high = ("low", "high") if step == NZ // 2 else ("all", "all")
        send(base, rblock(lane, 1 - step), low, device(0, 0, 1))
        send(base + 1, rblock(lane, step - 1), high, device(0, 0, -1))

    def z_arrive(lane, step):
        base = M_Z + lane * 8 + (step - 1) * 2
        low, high = ("low", "high") if step == NZ // 2 else ("all", "all")
        arrive(base, rblock(lane, -step), low)
        arrive(base + 1, rblock(lane, step), high)

    def x_step(step):
        base = M_X + (step - 1) * 2
        low, high = ("low", "high") if step == 2 else ("all", "all")
        send(base, pblock(1 - step, 0), low, device(1, 0, 0))
        send(base + 1, pblock(step - 1, 0), high, device(-1, 0, 0))

    def x_arrive(step):
        base = M_X + (step - 1) * 2
        low, high = ("low", "high") if step == 2 else ("all", "all")
        arrive(base, pblock(-step, 0), low)
        arrive(base + 1, pblock(step, 0), high)

    def y_step(dx, step):
        base = M_Y + (dx % NX) * 4 + (step - 1) * 2
        low, high = ("low", "high") if step == 2 else ("all", "all")
        send(base, pblock(dx, 1 - step), low, device(0, 1, 0))
        send(base + 1, pblock(dx, step - 1), high, device(0, -1, 0))

    def y_arrive(dx, step):
        base = M_Y + (dx % NX) * 4 + (step - 1) * 2
        low, high = ("low", "high") if step == 2 else ("all", "all")
        arrive(base, pblock(dx, -step), low)
        arrive(base + 1, pblock(dx, step), high)

    z_step(0, 1)

    bias[0] = jnp.zeros((ROWS, ROWS), F32)

    def set_bias(block, _):
        bias[block + 1] = block_bias(order_ref, len_ref, seq, block)
        return 0

    lax.fori_loop(0, 2 * NZ, set_bias, 0)
    acc[...] = jnp.zeros_like(acc)

    def event_0():
        for d in range(1, NZ):
            there = kv.at[own_prompt, pl.ds(pl.multiple_of(lax.rem(z - d + NZ, NZ) * 16, 16), 16), :]
            copy(M_PIECE + d - 1, there, there, device(0, 0, 1)).wait_recv()
        y_step(0, 1)
        x_step(1)

    def event_1():
        arrive(M_EXCH, rblock(1, 0))
        z_step(1, 1)
        z_arrive(0, 1)
        z_step(0, 2)

    def event_2():
        y_arrive(0, 1)
        y_step(0, 2)
        x_arrive(1)
        x_step(2)
        y_step(1, 1)
        y_step(-1, 1)

    def event_3():
        y_arrive(0, 2)

    def event_4():
        z_arrive(1, 1)
        z_step(1, 2)

    def event_5():
        x_arrive(2)
        y_step(2, 1)

    def event_6():
        z_arrive(0, 2)
        z_step(0, 3)

    def event_7():
        y_arrive(1, 1)
        y_step(1, 2)

    def event_8():
        z_arrive(1, 2)
        z_step(1, 3)

    def event_9():
        y_arrive(-1, 1)
        y_step(-1, 2)

    def event_10():
        z_arrive(0, 3)
        z_step(0, 4)

    def event_11():
        y_arrive(1, 2)
        y_arrive(-1, 2)

    def event_12():
        y_arrive(2, 1)
        y_step(2, 2)

    def event_13():
        z_arrive(1, 3)
        z_step(1, 4)

    def event_14():
        y_arrive(2, 2)

    def event_15():
        z_arrive(0, 4)
        z_arrive(1, 4)

    units = [
        (event_0, own_block, own_prompt),
        (event_1, rblock(0, -1), rblock(0, 1)),
        (event_2, pblock(0, -1), pblock(0, 1)),
        (event_3, rblock(1, 0), pblock(0, 2)),
        (event_4, rblock(1, -1), rblock(1, 1)),
        (event_5, pblock(1, 0), pblock(-1, 0)),
        (event_6, rblock(0, -2), rblock(0, 2)),
        (event_7, pblock(1, -1), pblock(1, 1)),
        (event_8, rblock(1, -2), rblock(1, 2)),
        (event_9, pblock(-1, -1), pblock(-1, 1)),
        (event_10, rblock(0, -3), rblock(0, 3)),
        (event_11, pblock(1, 2), pblock(-1, 2)),
        (event_12, pblock(2, -1), pblock(2, 1)),
        (event_13, rblock(1, -3), rblock(1, 3)),
        (event_14, pblock(2, 0), pblock(2, 2)),
        (event_15, rblock(0, 4), rblock(1, 4)),
    ]
    ones = jnp.ones((16, 2 * ROWS), BF16)

    def keep(unit, block, which):
        return pltpu.make_async_copy(kv.at[block], kept_ref.at[block], keep_sem.at[2 * unit + which])

    def pick(t, which):
        block = units[0][which]
        for i, unit in enumerate(units):
            block = jnp.where(t == i, unit[which], block)
        return block

    def work(t, _):
        for i, unit in enumerate(units):
            pl.when(t == i)(unit[0])
        one, two = pick(t, 1), pick(t, 2)
        keep(t, one, 0).start()
        keep(t, two, 1).start()
        bias_one = bias.at[jnp.maximum(one - (NPB - 1), 0)]
        bias_two = bias.at[jnp.maximum(two - (NPB - 1), 0)]

        def scores(h):
            k = jnp.concatenate(
                [kv[one, :, h * HD : (h + 1) * HD], kv[two, :, h * HD : (h + 1) * HD]], axis=0
            )
            return jnp.dot(jnp.concatenate([k, k], axis=1), qa[h], preferred_element_type=F32)

        def weights(s):
            b = jnp.concatenate([bias_one[...], bias_two[...]], axis=0)
            s = jnp.concatenate([s[:, g * ROWS : (g + 1) * ROWS] + b for g in range(GW)], axis=1)
            return jnp.exp2(s).astype(BF16)

        def mix(h, p):
            column = HALF + h * HD
            v = jnp.concatenate(
                [kv[one, :, column : column + HD].T, kv[two, :, column : column + HD].T], axis=1
            )
            acc[h] += jnp.dot(jnp.concatenate([v, ones], axis=0), p, preferred_element_type=F32)

        s, p = {0: scores(0)}, {}
        for h in range(KVH + 1):
            if h + 1 < KVH:
                s[h + 1] = scores(h + 1)
            if h >= 1:
                mix(h - 1, p.pop(h - 1))
            if h < KVH:
                p[h] = weights(s.pop(h))
        return 0

    lax.fori_loop(0, len(units), work, 0)

    scale_row = row_scale(order_ref, len_ref, tags_ref, weight_ref, seq)
    bad = jnp.zeros((1, ROWS), F32)
    for h in range(KVH):
        for g in range(GW):
            columns = slice(g * ROWS, (g + 1) * ROWS)
            total = acc[h, HD : HD + 1, columns]
            bad = jnp.where((total >= LEAST) & (total <= MOST), bad, 1.0)
            mixed = (acc[h, 0:HD, columns] * (scale_row / total)).astype(BF16)
            column = (h * GW + g) * HD
            out_ref[:, column : column + HD] = mixed.T
    bad_ref[...] = bad

    for t, unit in enumerate(units):
        keep(t, unit[1], 0).wait()
        keep(t, unit[2], 1).wait()
    for d in range(1, NZ):
        copy(M_PIECE + d - 1, piece_ref, mine, device(0, 0, d)).wait_send()
    for message, part in started.items():
        here = part_of(own_block, part)
        copy(message, here, here, device(0, 0, 1)).wait_send()


def check_rows(len_ref, order_ref, tags_ref, weight_ref, bad_ref, q_ref, kept_ref, first_ref, out_ref, q, kv, out, sem):
    del first_ref
    seq = lax.axis_index("seq")

    @pl.when(jnp.max(bad_ref[...]) > 0.0)
    def redo():
        for src, dst in ((q_ref, q), (kept_ref, kv)):
            fetch = pltpu.make_async_copy(src, dst, sem)
            fetch.start()
            fetch.wait()
        scale_row = row_scale(order_ref, len_ref, tags_ref, weight_ref, seq)

        def head(index, _):
            columns = pl.ds(pl.multiple_of(index * HD, HD), HD)
            kv_head = lax.div(index, GW)
            key_columns = pl.ds(pl.multiple_of(kv_head * HD, HD), HD)
            value_columns = pl.ds(pl.multiple_of(HALF + kv_head * HD, HD), HD)
            queries = q[:, columns]

            def scores(block):
                s = lax.dot_general(
                    kv[block, :, key_columns], queries, (((1,), (1,)), ((), ())), preferred_element_type=F32
                )
                b = block_bias(order_ref, len_ref, seq, jnp.maximum(block - NPB, 0))
                return jnp.where(block < NPB, s * SCALE, s * SCALE + b)

            def top_of(block, top):
                return jnp.maximum(top, jnp.max(scores(block), axis=0, keepdims=True))

            blocks = kv.shape[0]
            top = lax.fori_loop(0, blocks, top_of, jnp.full((1, ROWS), -jnp.inf, F32))

            def add(block, carry):
                total, mixed = carry
                w = jnp.exp2(scores(block) - top)
                total += jnp.sum(w, axis=0, keepdims=True)
                mixed += jnp.dot(kv[block, :, value_columns].T, w.astype(BF16), preferred_element_type=F32)
                return total, mixed

            total, mixed = lax.fori_loop(
                0, blocks, add, (jnp.zeros((1, ROWS), F32), jnp.zeros((HD, ROWS), F32))
            )
            out[:, columns] = (mixed * (scale_row / total)).astype(BF16).T
            return 0

        lax.fori_loop(0, H, head, 0)
        store = pltpu.make_async_copy(out, out_ref, sem)
        store.start()
        store.wait()


def shards(resp_q, resp_kv, prompt_kv, resp_len, block_order, tags, ver_weight):
    blocks = NPB + 2 * NZ
    smem = pl.BlockSpec(memory_space=pltpu.SMEM)
    vmem = pl.BlockSpec(memory_space=pltpu.VMEM)
    anywhere = pl.BlockSpec(memory_space=pl.ANY)
    scalars = (resp_len, block_order, tags, ver_weight)
    queries = resp_q[0]
    width = 2 * HALF
    keys = blocks * ROWS
    attended, bad, kept = pl.pallas_call(
        gather_attend,
        out_shape=(
            jax.ShapeDtypeStruct((ROWS, H * HD), BF16),
            jax.ShapeDtypeStruct((1, ROWS), F32),
            jax.ShapeDtypeStruct((blocks, ROWS, width), BF16),
        ),
        in_specs=[smem] * 4 + [vmem] * 3,
        out_specs=(vmem, vmem, anywhere),
        scratch_shapes=[
            pltpu.VMEM((blocks, ROWS, width), BF16),
            pltpu.VMEM((KVH, 2 * HD, GW * ROWS), BF16),
            pltpu.VMEM((KVH, HD + 16, GW * ROWS), F32),
            pltpu.VMEM((2 * NZ + 1, ROWS, ROWS), F32),
            pltpu.SemaphoreType.DMA((N_MSG,)),
            pltpu.SemaphoreType.DMA((N_MSG,)),
            pltpu.SemaphoreType.DMA((blocks,)),
        ],
        compiler_params=pltpu.CompilerParams(
            collective_id=0, has_side_effects=True, vmem_limit_bytes=48 * 2**20
        ),
        cost_estimate=pl.CostEstimate(
            flops=4 * ROWS * H * HD * keys, bytes_accessed=2 * keys * width, transcendentals=ROWS * H * keys
        ),
    )(*scalars, queries, resp_kv[0], prompt_kv)
    final = pl.pallas_call(
        check_rows,
        out_shape=jax.ShapeDtypeStruct((ROWS, H * HD), BF16),
        in_specs=[smem] * 4 + [vmem] + [anywhere] * 3,
        out_specs=anywhere,
        scratch_shapes=[
            pltpu.VMEM((ROWS, H * HD), BF16),
            pltpu.VMEM((blocks, ROWS, width), BF16),
            pltpu.VMEM((ROWS, H * HD), BF16),
            pltpu.SemaphoreType.DMA,
        ],
        input_output_aliases={7: 0},
        compiler_params=pltpu.CompilerParams(vmem_limit_bytes=32 * 2**20),
    )(*scalars, bad, queries, kept, attended)
    return final[None]


def solution(mesh):
    in_specs = (
        P(("grp", "smp"), "seq", None),
        P(("grp", "smp"), "seq", None),
        P(("grp", "smp", "seq"), None),
        P(("grp", "smp")),
        P("grp"),
        P(("grp", "smp"), "seq"),
        P(),
    )
    out_specs = P(("grp", "smp"), "seq", None)
    return jax.shard_map(shards, mesh=mesh, in_specs=in_specs, out_specs=out_specs, check_vma=False)
```

```python
import functools
import math

import jax
import jax.numpy as jnp
from jax import lax
from jax.experimental import pallas as pl
from jax.experimental.pallas import tpu as pltpu
from jax.sharding import PartitionSpec as P

MESH = pl.DeviceIdType.MESH
F32 = jnp.float32
BF16 = jnp.bfloat16
H = 32
KVH = 4
HD = 128
GW = H // KVH
HALF = KVH * HD
ROWS = 128
BLK = 64
NX, NY, NZ = 4, 4, 8
NPB = NX * NY
SCALE = HD**-0.5 * math.log2(math.e)
LEAST, MOST = 2.0**-80, 2.0**100

PIECE = 16
PART = 256
WHOLE, FEW, MOST_OF = slice(0, 4), slice(0, 1), slice(1, 4)
KINDS = {"few": (FEW, 0), "own": (MOST_OF, 0), "other": (MOST_OF, 1)}
ALL, LOW, HIGH = (0, ROWS), (0, ROWS // 2), (ROWS // 2, ROWS // 2)
NEAR, FAR = (0, 5 * PIECE), (5 * PIECE, 3 * PIECE)
N_MSG = 64
PARTS = 4


def positions(order_ref, block, along, shape):
    index = lax.broadcasted_iota(jnp.int32, shape, along)
    first, second = order_ref[2 * block], order_ref[2 * block + 1]
    return jnp.where(index < BLK, first * BLK + index, second * BLK + index - BLK)


def row_scale(order_ref, len_ref, tags_ref, weight_ref, seq):
    shape = (1, ROWS)
    query_pos = positions(order_ref, seq, 1, shape)
    picked = []
    for k in range(2):
        value = jnp.float32(0.0)
        for v in range(weight_ref.shape[0]):
            value = jnp.where(tags_ref[0, k] == v, weight_ref[v], value)
        picked.append(value)
    index = lax.broadcasted_iota(jnp.int32, shape, 1)
    weight = jnp.where(index < BLK, picked[0], picked[1])
    return jnp.where(query_pos < len_ref[0], weight, 0.0)


def block_bias(order_ref, len_ref, seq, block):
    shape = (ROWS, ROWS)
    query_pos = positions(order_ref, seq, 1, shape)
    key_pos = positions(order_ref, block, 0, shape)
    allowed = (key_pos <= query_pos) & (key_pos < len_ref[0])
    return jnp.where(allowed, 0.0, -jnp.inf).astype(F32)


def gather_attend(
    len_in, order_in, tags_in, weight_in, q_in, own_in, piece_in,
    out_ref, bad_ref, kept_ref,
    len_ref, order_ref, tags_ref, weight_ref, q_ref,
    kv, qa, acc, bias, load_sem, send_sem, recv_sem, keep_sem,
):
    grp, smp, seq = lax.axis_index("grp"), lax.axis_index("smp"), lax.axis_index("seq")
    x_hi, z = lax.div(seq, NZ), lax.rem(seq, NZ)
    x_lo, y = lax.div(smp, NY), lax.rem(smp, NY)
    x = x_hi * 2 + x_lo

    def device(dx, dy, dz):
        xx, yy, zz = lax.rem(x + dx + NX, NX), lax.rem(y + dy + NY, NY), lax.rem(z + dz + NZ, NZ)
        return (grp, lax.rem(xx, 2) * NY + yy, lax.div(xx, 2) * NZ + zz)

    def rblock(lane, dz):
        column = x_hi if lane == 0 else 1 - x_hi
        return NPB + column * NZ + lax.rem(z + dz + NZ, NZ)

    def pblock(dx, dy):
        return lax.rem(x + dx + NX, NX) * NY + lax.rem(y + dy + NY, NY)

    peers = [device(0, 0, d) for d in range(1, NZ)]
    peers += [device(d, 0, 0) for d in range(1, NX)] + [device(0, 1, 0), device(0, -1, 0)]
    barrier = pltpu.get_barrier_semaphore()
    for peer in peers:
        pl.semaphore_signal(barrier, inc=1, device_id=peer, device_id_type=MESH)

    own_block, own_prompt = rblock(0, 0), pblock(0, 0)
    pairs = [(piece_in.at[:, k * PART : (k + 1) * PART], kv.at[k, own_prompt, 0:PIECE, :]) for k in range(4)]
    pairs += [(own_in.at[:, k * PART : (k + 1) * PART], kv.at[k, own_block]) for k in range(4)]
    pairs += [(q_in, q_ref), (len_in, len_ref), (order_in, order_ref), (tags_in, tags_ref), (weight_in, weight_ref)]
    loads = [pltpu.make_async_copy(src, dst, load_sem.at[i]) for i, (src, dst) in enumerate(pairs)]
    for load in loads:
        load.start()

    sent = {}
    numbers = {}

    def number(name):
        return numbers.setdefault(name, len(numbers))

    def piece_of(which, block, rows):
        start, size = rows
        return kv.at[which, block, pl.ds(start, size), :]

    def copy(name, ref, to):
        m = number(name)
        return pltpu.make_async_remote_copy(
            src_ref=ref[0], dst_ref=ref[1], send_sem=send_sem.at[m], recv_sem=recv_sem.at[m],
            device_id=to, device_id_type=MESH,
        )

    def send(name, which, block, rows, to, there=None):
        src = piece_of(which, block, rows)
        dst = src if there is None else piece_of(which, block, there)
        sent[name] = (which, rows)
        copy(name, (src, dst), to).start()

    def arrive(name, which, block, rows=ALL):
        here = piece_of(which, block, rows)
        copy(name, (here, here), device(0, 0, 1)).wait_recv()

    def z_step(kind, step):
        which, lane = KINDS[kind]
        low, high = (LOW, HIGH) if step == NZ // 2 else (ALL, ALL)
        send((kind, step, 1), which, rblock(lane, 1 - step), low, device(0, 0, 1))
        send((kind, step, -1), which, rblock(lane, step - 1), high, device(0, 0, -1))

    def z_arrive(kind, step):
        which, lane = KINDS[kind]
        low, high = (LOW, HIGH) if step == NZ // 2 else (ALL, ALL)
        arrive((kind, step, 1), which, rblock(lane, -step), low)
        arrive((kind, step, -1), which, rblock(lane, step), high)

    def x_step(step, rows, tag=0):
        low, high = (LOW, HIGH) if step == 2 else (rows, rows)
        send(("x", step, 1, tag), WHOLE, pblock(1 - step, 0), low, device(1, 0, 0))
        send(("x", step, -1, tag), WHOLE, pblock(step - 1, 0), high, device(-1, 0, 0))

    def x_arrive(step, rows, tag=0):
        low, high = (LOW, HIGH) if step == 2 else (rows, rows)
        arrive(("x", step, 1, tag), WHOLE, pblock(-step, 0), low)
        arrive(("x", step, -1, tag), WHOLE, pblock(step, 0), high)

    def y_step(dx, step, rows=ALL, tag=0):
        low, high = (LOW, HIGH) if step == 2 else (rows, rows)
        send(("y", dx, step, 1, tag), WHOLE, pblock(dx, 1 - step), low, device(0, 1, 0))
        send(("y", dx, step, -1, tag), WHOLE, pblock(dx, step - 1), high, device(0, -1, 0))

    def y_arrive(dx, step, rows=ALL, tag=0):
        low, high = (LOW, HIGH) if step == 2 else (rows, rows)
        arrive(("y", dx, step, 1, tag), WHOLE, pblock(dx, -step), low)
        arrive(("y", dx, step, -1, tag), WHOLE, pblock(dx, step), high)

    def cross(step):
        for d in sorted({-step, step} if step < NZ // 2 else {step}):
            send(("cross", d), FEW, rblock(0, d), ALL, device(2, 0, 0))

    def cross_arrive(step):
        for d in sorted({-step, step} if step < NZ // 2 else {step}):
            arrive(("cross", d), FEW, rblock(1, d))

    loads[8].wait()
    for h in range(KVH):
        for g in range(GW):
            column = (h * GW + g) * HD
            scaled = q_ref[:, column : column + HD].T.astype(F32) * SCALE
            high = scaled.astype(BF16)
            qa[h, 0:HD, g * ROWS : (g + 1) * ROWS] = high
            qa[h, HD : 2 * HD, g * ROWS : (g + 1) * ROWS] = (scaled - high.astype(F32)).astype(BF16)
    for load in loads[:8] + loads[9:]:
        load.wait()

    pl.semaphore_wait(barrier, len(peers))

    slots = {0: 0, -1: 1, 1: 2, -2: 3, 2: 4, -3: 5, 3: 6, 4: 7}

    def slot(d):
        return (slots[d] * PIECE, PIECE)

    for d in (1, -1, 2, -2, 3, -3, 4):
        send(("piece", d), WHOLE, own_prompt, slot(0), device(0, 0, d), there=slot(-d if d < 4 else 4))
    send("most", MOST_OF, own_block, ALL, device(2, 0, 0))
    cross(0)
    z_step("few", 1)
    z_step("own", 1)

    bias[0] = jnp.zeros((ROWS, ROWS), F32)

    def set_bias(block, _):
        bias[block + 1] = block_bias(order_ref, len_ref, seq, block)
        return 0

    lax.fori_loop(0, 2 * NZ, set_bias, 0)
    acc[...] = jnp.zeros_like(acc)

    def pieces_arrive(distances):
        for d in distances:
            arrive(("piece", d), WHOLE, own_prompt, slot(-d if d < 4 else 4))

    def event_0():
        pieces_arrive((1, -1, 2, -2))
        y_step(0, 1, NEAR, 0)
        x_step(1, NEAR, 0)
        pieces_arrive((3, -3, 4))
        y_step(0, 1, FAR, 1)
        x_step(1, FAR, 1)

    def event_1():
        z_arrive("few", 1)
        z_step("few", 2)
        cross(1)
        arrive("most", MOST_OF, rblock(1, 0))
        z_step("other", 1)
        y_arrive(0, 1, NEAR, 0)
        y_arrive(0, 1, FAR, 1)
        y_step(0, 2)

    def event_2():
        z_arrive("own", 1)
        z_step("own", 2)
        x_arrive(1, NEAR, 0)
        x_arrive(1, FAR, 1)
        x_step(2, ALL)
        y_step(1, 1)
        y_step(-1, 1)
        z_arrive("few", 2)
        z_step("few", 3)
        cross(2)

    def event_3():
        pass

    def event_4():
        cross_arrive(0)
        y_arrive(0, 2)

    def event_5():
        z_arrive("other", 1)
        z_step("other", 2)
        cross_arrive(1)

    def event_6():
        x_arrive(2, ALL)
        y_step(2, 1)
        z_arrive("own", 2)
        z_step("own", 3)

    def event_7():
        y_arrive(1, 1)
        y_step(1, 2)
        z_arrive("few", 3)
        z_step("few", 4)
        cross(3)

    def event_8():
        z_arrive("other", 2)
        z_step("other", 3)
        cross_arrive(2)

    def event_9():
        y_arrive(-1, 1)
        y_step(-1, 2)

    def event_10():
        z_arrive("own", 3)
        z_step("own", 4)

    def event_11():
        z_arrive("few", 4)
        cross(4)
        y_arrive(2, 1)
        y_step(2, 2)

    def event_12():
        z_arrive("other", 3)
        z_step("other", 4)
        cross_arrive(3)

    def event_13():
        y_arrive(1, 2)
        y_arrive(-1, 2)

    def event_14():
        z_arrive("own", 4)
        z_arrive("other", 4)
        cross_arrive(4)

    def event_15():
        y_arrive(2, 2)

    units = [
        (event_0, own_block, own_prompt),
        (event_1, pblock(0, -1), pblock(0, 1)),
        (event_2, rblock(0, -1), rblock(0, 1)),
        (event_3, pblock(1, 0), pblock(-1, 0)),
        (event_4, rblock(1, 0), pblock(0, 2)),
        (event_5, rblock(1, -1), rblock(1, 1)),
        (event_6, rblock(0, -2), rblock(0, 2)),
        (event_7, pblock(1, -1), pblock(1, 1)),
        (event_8, rblock(1, -2), rblock(1, 2)),
        (event_9, pblock(-1, -1), pblock(-1, 1)),
        (event_10, rblock(0, -3), rblock(0, 3)),
        (event_11, pblock(2, -1), pblock(2, 1)),
        (event_12, rblock(1, -3), rblock(1, 3)),
        (event_13, pblock(1, 2), pblock(-1, 2)),
        (event_14, rblock(0, 4), rblock(1, 4)),
        (event_15, pblock(2, 0), pblock(2, 2)),
    ]
    ones = jnp.ones((16, 2 * ROWS), BF16)

    def keep(unit, block, which):
        return pltpu.make_async_copy(kv.at[:, block], kept_ref.at[:, block], keep_sem.at[2 * unit + which])

    def pick(t, which):
        block = units[0][which]
        for i, unit in enumerate(units):
            block = jnp.where(t == i, unit[which], block)
        return block

    def work(t, _):
        for i, unit in enumerate(units):
            pl.when(t == i)(unit[0])
        one, two = pick(t, 1), pick(t, 2)
        keep(t, one, 0).start()
        keep(t, two, 1).start()
        bias_one = bias.at[jnp.maximum(one - (NPB - 1), 0)]
        bias_two = bias.at[jnp.maximum(two - (NPB - 1), 0)]

        def scores(h):
            part, columns = h // 2, slice(h % 2 * HD, (h % 2 + 1) * HD)
            k = jnp.concatenate([kv[part, one, :, columns], kv[part, two, :, columns]], axis=0)
            return jnp.dot(jnp.concatenate([k, k], axis=1), qa[h], preferred_element_type=F32)

        def weights(s):
            b = jnp.concatenate([bias_one[...], bias_two[...]], axis=0)
            s = jnp.concatenate([s[:, g * ROWS : (g + 1) * ROWS] + b for g in range(GW)], axis=1)
            return jnp.exp2(s).astype(BF16)

        def mix(h, p):
            part, columns = 2 + h // 2, slice(h % 2 * HD, (h % 2 + 1) * HD)
            v = jnp.concatenate([kv[part, one, :, columns].T, kv[part, two, :, columns].T], axis=1)
            acc[h] += jnp.dot(jnp.concatenate([v, ones], axis=0), p, preferred_element_type=F32)

        s, p = {0: scores(0)}, {}
        for h in range(KVH + 1):
            if h + 1 < KVH:
                s[h + 1] = scores(h + 1)
            if h >= 1:
                mix(h - 1, p.pop(h - 1))
            if h < KVH:
                p[h] = weights(s.pop(h))
        return 0

    lax.fori_loop(0, len(units), work, 0)

    scale_row = row_scale(order_ref, len_ref, tags_ref, weight_ref, seq)
    bad = jnp.zeros((1, ROWS), F32)
    for h in range(KVH):
        for g in range(GW):
            columns = slice(g * ROWS, (g + 1) * ROWS)
            total = acc[h, HD : HD + 1, columns]
            bad = jnp.where((total >= LEAST) & (total <= MOST), bad, 1.0)
            mixed = (acc[h, 0:HD, columns] * (scale_row / total)).astype(BF16)
            column = (h * GW + g) * HD
            out_ref[:, column : column + HD] = mixed.T
    bad_ref[...] = bad

    for t, unit in enumerate(units):
        keep(t, unit[1], 0).wait()
        keep(t, unit[2], 1).wait()
    for name, (which, rows) in sent.items():
        here = piece_of(which, own_block, rows)
        copy(name, (here, here), device(0, 0, 1)).wait_send()


def check_rows(len_ref, order_ref, tags_ref, weight_ref, bad_ref, q_ref, kept_ref, first_ref, out_ref, q, kv, out, sem, pass_sem):
    seq = lax.axis_index("seq")
    parts = [slice(i * ROWS // PARTS, (i + 1) * ROWS // PARTS) for i in range(PARTS)]
    into = [pltpu.make_async_copy(first_ref.at[p], out.at[p], pass_sem.at[0, i]) for i, p in enumerate(parts)]
    onto = [pltpu.make_async_copy(out.at[p], out_ref.at[p], pass_sem.at[1, i]) for i, p in enumerate(parts)]
    for load in into:
        load.start()
    for load, store in zip(into, onto):
        load.wait()
        store.start()
    bad = jnp.max(bad_ref[...])
    for store in onto:
        store.wait()

    @pl.when(bad > 0.0)
    def redo():
        for src, dst in ((q_ref, q), (kept_ref, kv)):
            fetch = pltpu.make_async_copy(src, dst, sem)
            fetch.start()
            fetch.wait()
        scale_row = row_scale(order_ref, len_ref, tags_ref, weight_ref, seq)

        def head(index, _):
            columns = pl.ds(pl.multiple_of(index * HD, HD), HD)
            kv_head = lax.div(index, GW)
            part = lax.div(kv_head, 2)
            kv_columns = pl.ds(pl.multiple_of(lax.rem(kv_head, 2) * HD, HD), HD)
            queries = q[:, columns]

            def scores(block):
                s = lax.dot_general(
                    kv[part, block, :, kv_columns], queries, (((1,), (1,)), ((), ())), preferred_element_type=F32
                )
                b = block_bias(order_ref, len_ref, seq, jnp.maximum(block - NPB, 0))
                return jnp.where(block < NPB, s * SCALE, s * SCALE + b)

            def top_of(block, top):
                return jnp.maximum(top, jnp.max(scores(block), axis=0, keepdims=True))

            blocks = kv.shape[1]
            top = lax.fori_loop(0, blocks, top_of, jnp.full((1, ROWS), -jnp.inf, F32))

            def add(block, carry):
                total, mixed = carry
                w = jnp.exp2(scores(block) - top)
                total += jnp.sum(w, axis=0, keepdims=True)
                mixed += jnp.dot(kv[2 + part, block, :, kv_columns].T, w.astype(BF16), preferred_element_type=F32)
                return total, mixed

            total, mixed = lax.fori_loop(
                0, blocks, add, (jnp.zeros((1, ROWS), F32), jnp.zeros((HD, ROWS), F32))
            )
            out[:, columns] = (mixed * (scale_row / total)).astype(BF16).T
            return 0

        lax.fori_loop(0, H, head, 0)
        store = pltpu.make_async_copy(out, out_ref, sem)
        store.start()
        store.wait()


def shards(resp_q, resp_kv, prompt_kv, resp_len, block_order, tags, ver_weight):
    blocks = NPB + 2 * NZ
    smem = pl.BlockSpec(memory_space=pltpu.SMEM)
    vmem = pl.BlockSpec(memory_space=pltpu.VMEM)
    hbm = pl.BlockSpec(memory_space=pltpu.HBM)
    scalars = (resp_len, block_order, tags, ver_weight)
    queries = resp_q[0]
    kv_shape = (4, blocks, ROWS, PART)
    keys = blocks * ROWS
    attended, bad, kept = pl.pallas_call(
        gather_attend,
        out_shape=(
            jax.ShapeDtypeStruct((ROWS, H * HD), BF16),
            jax.ShapeDtypeStruct((1, ROWS), F32),
            jax.ShapeDtypeStruct(kv_shape, BF16),
        ),
        in_specs=[hbm] * 7,
        out_specs=(vmem, vmem, hbm),
        scratch_shapes=[pltpu.SMEM(a.shape, a.dtype) for a in scalars]
        + [
            pltpu.VMEM((ROWS, H * HD), BF16),
            pltpu.VMEM(kv_shape, BF16),
            pltpu.VMEM((KVH, 2 * HD, GW * ROWS), BF16),
            pltpu.VMEM((KVH, HD + 16, GW * ROWS), F32),
            pltpu.VMEM((2 * NZ + 1, ROWS, ROWS), F32),
            pltpu.SemaphoreType.DMA((13,)),
            pltpu.SemaphoreType.DMA((N_MSG,)),
            pltpu.SemaphoreType.DMA((N_MSG,)),
            pltpu.SemaphoreType.DMA((blocks,)),
        ],
        compiler_params=pltpu.CompilerParams(
            collective_id=0, has_side_effects=True, vmem_limit_bytes=60 * 2**20
        ),
        cost_estimate=pl.CostEstimate(
            flops=4 * ROWS * H * HD * keys, bytes_accessed=4 * keys * HALF, transcendentals=ROWS * H * keys
        ),
    )(*scalars, queries, resp_kv[0], prompt_kv)
    final = pl.pallas_call(
        check_rows,
        out_shape=jax.ShapeDtypeStruct((ROWS, H * HD), BF16),
        in_specs=[smem] * 4 + [vmem] + [hbm] * 2 + [pl.BlockSpec(memory_space=pl.ANY)],
        out_specs=hbm,
        scratch_shapes=[
            pltpu.VMEM((ROWS, H * HD), BF16),
            pltpu.VMEM(kv_shape, BF16),
            pltpu.VMEM((ROWS, H * HD), BF16),
            pltpu.SemaphoreType.DMA,
            pltpu.SemaphoreType.DMA((2, PARTS)),
        ],
        compiler_params=pltpu.CompilerParams(vmem_limit_bytes=60 * 2**20),
    )(*scalars, bad, queries, kept, attended)
    return final[None]


def solution(mesh):
    in_specs = (
        P(("grp", "smp"), "seq", None),
        P(("grp", "smp"), "seq", None),
        P(("grp", "smp", "seq"), None),
        P(("grp", "smp")),
        P("grp"),
        P(("grp", "smp"), "seq"),
        P(),
    )
    out_specs = P(("grp", "smp"), "seq", None)
    return jax.shard_map(shards, mesh=mesh, in_specs=in_specs, out_specs=out_specs, check_vma=False)
```

```python
import functools
import math

import jax
import jax.numpy as jnp
from jax import lax
from jax.experimental import pallas as pl
from jax.experimental.pallas import tpu as pltpu
from jax.sharding import PartitionSpec as P

MESH = pl.DeviceIdType.MESH
F32 = jnp.float32
BF16 = jnp.bfloat16
H = 32
KVH = 4
HD = 128
GW = H // KVH
HALF = KVH * HD
ROWS = 128
BLK = 64
NX, NY, NZ = 4, 4, 8
NPB = NX * NY
SCALE = HD**-0.5 * math.log2(math.e)
LEAST, MOST = 2.0**-80, 2.0**100

PIECE = 16
PARTS = 2 * KVH
WHOLE, FEW, MOST_OF = slice(0, PARTS), slice(0, 3), slice(3, PARTS)
KINDS = {"few": (FEW, 0), "own": (MOST_OF, 0), "other": (MOST_OF, 1)}
ALL, LOW, HIGH = (0, ROWS), (0, ROWS // 2), (ROWS // 2, ROWS // 2)
NEAR, FAR = (0, 5 * PIECE), (5 * PIECE, 3 * PIECE)
N_MSG = 80
N_PASS = 8


def positions(order_ref, block, along, shape):
    index = lax.broadcasted_iota(jnp.int32, shape, along)
    first, second = order_ref[2 * block], order_ref[2 * block + 1]
    return jnp.where(index < BLK, first * BLK + index, second * BLK + index - BLK)


def row_scale(order_ref, len_ref, tags_ref, weight_ref, seq):
    shape = (1, ROWS)
    query_pos = positions(order_ref, seq, 1, shape)
    picked = []
    for k in range(2):
        value = jnp.float32(0.0)
        for v in range(weight_ref.shape[0]):
            value = jnp.where(tags_ref[0, k] == v, weight_ref[v], value)
        picked.append(value)
    index = lax.broadcasted_iota(jnp.int32, shape, 1)
    weight = jnp.where(index < BLK, picked[0], picked[1])
    return jnp.where(query_pos < len_ref[0], weight, 0.0)


def block_bias(order_ref, len_ref, seq, block):
    shape = (ROWS, ROWS)
    query_pos = positions(order_ref, seq, 1, shape)
    key_pos = positions(order_ref, block, 0, shape)
    allowed = (key_pos <= query_pos) & (key_pos < len_ref[0])
    return jnp.where(allowed, 0.0, -jnp.inf).astype(F32)


def gather_attend(
    len_in, order_in, tags_in, weight_in, q_in, own_in, piece_in,
    out_hbm, bad_ref, kept_ref,
    len_ref, order_ref, tags_ref, weight_ref, q_ref,
    out_ref, kv, qa, acc, bias, load_sem, send_sem, recv_sem, keep_sem,
):
    grp, smp, seq = lax.axis_index("grp"), lax.axis_index("smp"), lax.axis_index("seq")
    x_hi, z = lax.div(seq, NZ), lax.rem(seq, NZ)
    x_lo, y = lax.div(smp, NY), lax.rem(smp, NY)
    x = x_hi * 2 + x_lo

    def device(dx, dy, dz):
        xx, yy, zz = lax.rem(x + dx + NX, NX), lax.rem(y + dy + NY, NY), lax.rem(z + dz + NZ, NZ)
        return (grp, lax.rem(xx, 2) * NY + yy, lax.div(xx, 2) * NZ + zz)

    def rblock(lane, dz):
        column = x_hi if lane == 0 else 1 - x_hi
        return NPB + column * NZ + lax.rem(z + dz + NZ, NZ)

    def pblock(dx, dy):
        return lax.rem(x + dx + NX, NX) * NY + lax.rem(y + dy + NY, NY)

    peers = [device(0, 0, d) for d in range(1, NZ)]
    peers += [device(d, 0, 0) for d in range(1, NX)] + [device(0, 1, 0), device(0, -1, 0)]
    barrier = pltpu.get_barrier_semaphore()
    for peer in peers:
        pl.semaphore_signal(barrier, inc=1, device_id=peer, device_id_type=MESH)

    own_block, own_prompt = rblock(0, 0), pblock(0, 0)
    pairs = [(piece_in.at[:, k * HD : (k + 1) * HD], kv.at[k, own_prompt, 0:PIECE, :]) for k in range(PARTS)]
    pairs += [(own_in.at[:, k * HD : (k + 1) * HD], kv.at[k, own_block]) for k in range(PARTS)]
    pairs += [(q_in, q_ref), (len_in, len_ref), (order_in, order_ref), (tags_in, tags_ref), (weight_in, weight_ref)]
    loads = [pltpu.make_async_copy(src, dst, load_sem.at[i]) for i, (src, dst) in enumerate(pairs)]
    for load in loads:
        load.start()

    sent = {}
    numbers = {}

    def number(name):
        return numbers.setdefault(name, len(numbers))

    def piece_of(which, block, rows):
        start, size = rows
        return kv.at[which, block, pl.ds(start, size), :]

    def copy(name, ref, to):
        m = number(name)
        return pltpu.make_async_remote_copy(
            src_ref=ref[0], dst_ref=ref[1], send_sem=send_sem.at[m], recv_sem=recv_sem.at[m],
            device_id=to, device_id_type=MESH,
        )

    def send(name, which, block, rows, to, there=None):
        src = piece_of(which, block, rows)
        dst = src if there is None else piece_of(which, block, there)
        sent[name] = (which, rows)
        copy(name, (src, dst), to).start()

    def arrive(name, which, block, rows=ALL):
        here = piece_of(which, block, rows)
        copy(name, (here, here), device(0, 0, 1)).wait_recv()

    def z_step(kind, step):
        which, lane = KINDS[kind]
        low, high = (LOW, HIGH) if step == NZ // 2 else (ALL, ALL)
        send((kind, step, 1), which, rblock(lane, 1 - step), low, device(0, 0, 1))
        send((kind, step, -1), which, rblock(lane, step - 1), high, device(0, 0, -1))

    def z_arrive(kind, step):
        which, lane = KINDS[kind]
        low, high = (LOW, HIGH) if step == NZ // 2 else (ALL, ALL)
        arrive((kind, step, 1), which, rblock(lane, -step), low)
        arrive((kind, step, -1), which, rblock(lane, step), high)

    def x_step(step, rows, tag=0):
        low, high = (LOW, HIGH) if step == 2 else (rows, rows)
        send(("x", step, 1, tag), WHOLE, pblock(1 - step, 0), low, device(1, 0, 0))
        send(("x", step, -1, tag), WHOLE, pblock(step - 1, 0), high, device(-1, 0, 0))

    def x_arrive(step, rows, tag=0):
        low, high = (LOW, HIGH) if step == 2 else (rows, rows)
        arrive(("x", step, 1, tag), WHOLE, pblock(-step, 0), low)
        arrive(("x", step, -1, tag), WHOLE, pblock(step, 0), high)

    def y_step(dx, step, right=ALL, left=ALL, tag=0):
        send(("y", dx, step, 1, tag), WHOLE, pblock(dx, 1 - step), right, device(0, 1, 0))
        send(("y", dx, step, -1, tag), WHOLE, pblock(dx, step - 1), left, device(0, -1, 0))

    def y_arrive(dx, step, right=ALL, left=ALL, tag=0):
        arrive(("y", dx, step, 1, tag), WHOLE, pblock(dx, -step), right)
        arrive(("y", dx, step, -1, tag), WHOLE, pblock(dx, step), left)

    def far_step():
        for d in (1, -1):
            send(("far", d), WHOLE, pblock(0, 2), ALL, device(d, 0, 0))

    def far_arrive():
        for d in (1, -1):
            arrive(("far", d), WHOLE, pblock(-d, 2))

    def cross(step):
        for d in sorted({-step, step} if step < NZ // 2 else {step}):
            send(("cross", d), FEW, rblock(0, d), ALL, device(2, 0, 0))

    def cross_arrive(step):
        for d in sorted({-step, step} if step < NZ // 2 else {step}):
            arrive(("cross", d), FEW, rblock(1, d))

    for load in loads:
        load.wait()
    bias[0] = jnp.zeros((ROWS, ROWS), F32)

    def set_bias(block, _):
        bias[block + 1] = block_bias(order_ref, len_ref, seq, block)
        return 0

    lax.fori_loop(0, 2 * NZ, set_bias, 0)
    acc[...] = jnp.zeros_like(acc)

    pl.semaphore_wait(barrier, len(peers))

    slots = {0: 0, -1: 1, 1: 2, -2: 3, 2: 4, -3: 5, 3: 6, 4: 7}

    def slot(d):
        return (slots[d] * PIECE, PIECE)

    for d in (1, -1, 2, -2, 3, -3, 4):
        send(("piece", d), WHOLE, own_prompt, slot(0), device(0, 0, d), there=slot(-d if d < 4 else 4))
    send("most", MOST_OF, own_block, ALL, device(2, 0, 0))
    cross(0)
    z_step("few", 1)
    z_step("own", 1)

    for h in range(KVH):
        for g in range(GW):
            column = (h * GW + g) * HD
            scaled = q_ref[:, column : column + HD].T.astype(F32) * SCALE
            high = scaled.astype(BF16)
            qa[h, 0:HD, g * ROWS : (g + 1) * ROWS] = high
            qa[h, HD : 2 * HD, g * ROWS : (g + 1) * ROWS] = (scaled - high.astype(F32)).astype(BF16)
    def pieces_arrive(distances):
        for d in distances:
            arrive(("piece", d), WHOLE, own_prompt, slot(-d if d < 4 else 4))

    def event_0():
        pieces_arrive((1, -1, 2, -2))
        y_step(0, 1, NEAR, NEAR)
        x_step(1, NEAR)
        z_arrive("few", 1)
        z_step("few", 2)
        cross(1)
        arrive("most", MOST_OF, rblock(1, 0))
        z_step("other", 1)
        pieces_arrive((3, -3, 4))
        y_step(0, 1, FAR, FAR, 1)
        x_step(1, FAR, 1)

    def event_1():
        x_arrive(1, NEAR)
        y_step(1, 1, NEAR, NEAR)
        y_step(-1, 1, NEAR, NEAR)
        z_arrive("own", 1)
        z_step("own", 2)

    def event_2():
        y_arrive(0, 1, NEAR, NEAR)
        y_arrive(0, 1, FAR, FAR, 1)
        y_step(0, 2, LOW, HIGH)

    def event_3():
        z_arrive("few", 2)
        z_step("few", 3)
        cross(2)
        x_arrive(1, FAR, 1)
        x_step(2, ALL)
        y_step(1, 1, FAR, FAR, 1)
        y_step(-1, 1, FAR, FAR, 1)

    def event_4():
        z_arrive("other", 1)
        z_step("other", 2)
        cross_arrive(1)

    def event_5():
        z_arrive("own", 2)
        z_step("own", 3)

    def event_6():
        z_arrive("few", 3)
        z_step("few", 4)
        cross(3)
        y_arrive(0, 2, LOW, HIGH)
        far_step()
        cross_arrive(0)

    def event_7():
        x_arrive(2, ALL)
        y_step(2, 1, LOW, HIGH)
        y_step(2, 1, HIGH, LOW, 1)
        y_arrive(-1, 1, NEAR, NEAR)
        y_arrive(-1, 1, FAR, FAR, 1)

    def event_8():
        z_arrive("other", 2)
        z_step("other", 3)
        cross_arrive(2)

    def event_9():
        y_arrive(1, 1, NEAR, NEAR)
        y_arrive(1, 1, FAR, FAR, 1)

    def event_10():
        z_arrive("own", 3)
        z_step("own", 4)

    def event_11():
        z_arrive("few", 4)
        cross(4)
        y_arrive(2, 1, LOW, HIGH)
        y_step(2, 2, LOW, HIGH)
        y_arrive(2, 1, HIGH, LOW, 1)

    def event_12():
        z_arrive("other", 3)
        z_step("other", 4)
        cross_arrive(3)

    def event_13():
        far_arrive()

    def event_14():
        y_arrive(2, 2, LOW, HIGH)

    def event_15():
        z_arrive("own", 4)
        z_arrive("other", 4)
        cross_arrive(4)

    units = [
        (event_0, own_block, own_prompt),
        (event_1, rblock(0, -1), rblock(0, 1)),
        (event_2, pblock(0, -1), pblock(0, 1)),
        (event_3, pblock(1, 0), pblock(-1, 0)),
        (event_4, rblock(1, -1), rblock(1, 1)),
        (event_5, rblock(0, -2), rblock(0, 2)),
        (event_6, rblock(1, 0), pblock(0, 2)),
        (event_7, pblock(-1, -1), pblock(-1, 1)),
        (event_8, rblock(1, -2), rblock(1, 2)),
        (event_9, pblock(1, -1), pblock(1, 1)),
        (event_10, rblock(0, -3), rblock(0, 3)),
        (event_11, pblock(2, -1), pblock(2, 1)),
        (event_12, rblock(1, -3), rblock(1, 3)),
        (event_13, pblock(1, 2), pblock(-1, 2)),
        (event_14, pblock(2, 0), pblock(2, 2)),
        (event_15, rblock(0, 4), rblock(1, 4)),
    ]
    ones = jnp.ones((16, 2 * ROWS), BF16)

    def keep(unit, block, which):
        return pltpu.make_async_copy(kv.at[:, block], kept_ref.at[:, block], keep_sem.at[2 * unit + which])

    def pick(t, which):
        block = units[0][which]
        for i, unit in enumerate(units):
            block = jnp.where(t == i, unit[which], block)
        return block

    def work(t, _):
        for i, unit in enumerate(units):
            pl.when(t == i)(unit[0])
        one, two = pick(t, 1), pick(t, 2)
        keep(t, one, 0).start()
        keep(t, two, 1).start()
        bias_one = bias.at[jnp.maximum(one - (NPB - 1), 0)]
        bias_two = bias.at[jnp.maximum(two - (NPB - 1), 0)]

        def scores(h):
            k = jnp.concatenate([kv[h, one], kv[h, two]], axis=0)
            return jnp.dot(jnp.concatenate([k, k], axis=1), qa[h], preferred_element_type=F32)

        def weights(s):
            b = jnp.concatenate([bias_one[...], bias_two[...]], axis=0)
            s = jnp.concatenate([s[:, g * ROWS : (g + 1) * ROWS] + b for g in range(GW)], axis=1)
            return jnp.exp2(s).astype(BF16)

        def mix(h, p):
            v = jnp.concatenate([kv[KVH + h, one].T, kv[KVH + h, two].T], axis=1)
            acc[h] += jnp.dot(jnp.concatenate([v, ones], axis=0), p, preferred_element_type=F32)

        s, p = {0: scores(0)}, {}
        for h in range(KVH + 1):
            if h + 1 < KVH:
                s[h + 1] = scores(h + 1)
            if h >= 1:
                mix(h - 1, p.pop(h - 1))
            if h < KVH:
                p[h] = weights(s.pop(h))
        return 0

    lax.fori_loop(0, len(units), work, 0)

    scale_row = row_scale(order_ref, len_ref, tags_ref, weight_ref, seq)
    bad = jnp.zeros((1, ROWS), F32)
    spans = [slice(h * GW * HD, (h + 1) * GW * HD) for h in range(KVH)]
    stores = [pltpu.make_async_copy(out_ref.at[:, c], out_hbm.at[:, c], load_sem.at[i]) for i, c in enumerate(spans)]
    for h in range(KVH):
        for g in range(GW):
            columns = slice(g * ROWS, (g + 1) * ROWS)
            total = acc[h, HD : HD + 1, columns]
            bad = jnp.where((total >= LEAST) & (total <= MOST), bad, 1.0)
            mixed = (acc[h, 0:HD, columns] * (scale_row / total)).astype(BF16)
            column = (h * GW + g) * HD
            out_ref[:, column : column + HD] = mixed.T
        stores[h].start()
    bad_ref[...] = bad

    for store in stores:
        store.wait()
    for t, unit in enumerate(units):
        keep(t, unit[1], 0).wait()
        keep(t, unit[2], 1).wait()
    for name, (which, rows) in sent.items():
        here = piece_of(which, own_block, rows)
        copy(name, (here, here), device(0, 0, 1)).wait_send()


def check_rows(
    len_in, order_in, tags_in, weight_in, bad_ref, q_ref, kept_ref, first_ref,
    out_ref,
    len_ref, order_ref, tags_ref, weight_ref, q, kv, out, sem, pass_sem,
):
    seq = lax.axis_index("seq")
    parts = [slice(i * ROWS // N_PASS, (i + 1) * ROWS // N_PASS) for i in range(N_PASS)]
    into = [pltpu.make_async_copy(first_ref.at[p], out.at[p], pass_sem.at[0, i]) for i, p in enumerate(parts)]
    onto = [pltpu.make_async_copy(out.at[p], out_ref.at[p], pass_sem.at[1, i]) for i, p in enumerate(parts)]
    for load in into:
        load.start()
    for load, store in zip(into, onto):
        load.wait()
        store.start()
    bad = jnp.max(bad_ref[...])
    for store in onto:
        store.wait()

    @pl.when(bad > 0.0)
    def redo():
        scalars = ((len_in, len_ref), (order_in, order_ref), (tags_in, tags_ref), (weight_in, weight_ref))
        for src, dst in ((q_ref, q), (kept_ref, kv), *scalars):
            fetch = pltpu.make_async_copy(src, dst, sem)
            fetch.start()
            fetch.wait()
        scale_row = row_scale(order_ref, len_ref, tags_ref, weight_ref, seq)

        def head(index, _):
            columns = pl.ds(pl.multiple_of(index * HD, HD), HD)
            kv_head = lax.div(index, GW)
            queries = q[:, columns]

            def scores(block):
                s = lax.dot_general(
                    kv[kv_head, block], queries, (((1,), (1,)), ((), ())), preferred_element_type=F32
                )
                b = block_bias(order_ref, len_ref, seq, jnp.maximum(block - NPB, 0))
                return jnp.where(block < NPB, s * SCALE, s * SCALE + b)

            def top_of(block, top):
                return jnp.maximum(top, jnp.max(scores(block), axis=0, keepdims=True))

            blocks = kv.shape[1]
            top = lax.fori_loop(0, blocks, top_of, jnp.full((1, ROWS), -jnp.inf, F32))

            def add(block, carry):
                total, mixed = carry
                w = jnp.exp2(scores(block) - top)
                total += jnp.sum(w, axis=0, keepdims=True)
                mixed += jnp.dot(kv[KVH + kv_head, block].T, w.astype(BF16), preferred_element_type=F32)
                return total, mixed

            total, mixed = lax.fori_loop(
                0, blocks, add, (jnp.zeros((1, ROWS), F32), jnp.zeros((HD, ROWS), F32))
            )
            out[:, columns] = (mixed * (scale_row / total)).astype(BF16).T
            return 0

        lax.fori_loop(0, H, head, 0)
        store = pltpu.make_async_copy(out, out_ref, sem)
        store.start()
        store.wait()


def shards(resp_q, resp_kv, prompt_kv, resp_len, block_order, tags, ver_weight):
    blocks = NPB + 2 * NZ
    vmem = pl.BlockSpec(memory_space=pltpu.VMEM)
    hbm = pl.BlockSpec(memory_space=pltpu.HBM)
    scalars = (resp_len, block_order, tags, ver_weight)
    queries = resp_q[0]
    kv_shape = (PARTS, blocks, ROWS, HD)
    keys = blocks * ROWS
    attended, bad, kept = pl.pallas_call(
        gather_attend,
        out_shape=(
            jax.ShapeDtypeStruct((ROWS, H * HD), BF16),
            jax.ShapeDtypeStruct((1, ROWS), F32),
            jax.ShapeDtypeStruct(kv_shape, BF16),
        ),
        in_specs=[hbm] * 7,
        out_specs=(hbm, vmem, hbm),
        scratch_shapes=[pltpu.SMEM(a.shape, a.dtype) for a in scalars]
        + [
            pltpu.VMEM((ROWS, H * HD), BF16),
            pltpu.VMEM((ROWS, H * HD), BF16),
            pltpu.VMEM(kv_shape, BF16),
            pltpu.VMEM((KVH, 2 * HD, GW * ROWS), BF16),
            pltpu.VMEM((KVH, HD + 16, GW * ROWS), F32),
            pltpu.VMEM((2 * NZ + 1, ROWS, ROWS), F32),
            pltpu.SemaphoreType.DMA((2 * PARTS + 5,)),
            pltpu.SemaphoreType.DMA((N_MSG,)),
            pltpu.SemaphoreType.DMA((N_MSG,)),
            pltpu.SemaphoreType.DMA((blocks,)),
        ],
        compiler_params=pltpu.CompilerParams(
            collective_id=0, has_side_effects=True, vmem_limit_bytes=60 * 2**20
        ),
        cost_estimate=pl.CostEstimate(
            flops=4 * ROWS * H * HD * keys, bytes_accessed=4 * keys * HALF, transcendentals=ROWS * H * keys
        ),
    )(*scalars, queries, resp_kv[0], prompt_kv)
    final = pl.pallas_call(
        check_rows,
        out_shape=jax.ShapeDtypeStruct((ROWS, H * HD), BF16),
        in_specs=[hbm] * 4 + [vmem] + [hbm] * 3,
        out_specs=hbm,
        scratch_shapes=[pltpu.SMEM(a.shape, a.dtype) for a in scalars]
        + [
            pltpu.VMEM((ROWS, H * HD), BF16),
            pltpu.VMEM(kv_shape, BF16),
            pltpu.VMEM((ROWS, H * HD), BF16),
            pltpu.SemaphoreType.DMA,
            pltpu.SemaphoreType.DMA((2, N_PASS)),
        ],
        compiler_params=pltpu.CompilerParams(vmem_limit_bytes=60 * 2**20),
    )(*scalars, bad, queries, kept, attended)
    return final[None]


def solution(mesh):
    in_specs = (
        P(("grp", "smp"), "seq", None),
        P(("grp", "smp"), "seq", None),
        P(("grp", "smp", "seq"), None),
        P(("grp", "smp")),
        P("grp"),
        P(("grp", "smp"), "seq"),
        P(),
    )
    out_specs = P(("grp", "smp"), "seq", None)
    return jax.shard_map(shards, mesh=mesh, in_specs=in_specs, out_specs=out_specs, check_vma=False)
```

```python
import functools
import math

import jax
import jax.numpy as jnp
from jax import lax
from jax.experimental import pallas as pl
from jax.experimental.pallas import tpu as pltpu
from jax.sharding import PartitionSpec as P

MESH = pl.DeviceIdType.MESH
F32 = jnp.float32
BF16 = jnp.bfloat16
H = 32
KVH = 4
HD = 128
GW = H // KVH
HALF = KVH * HD
ROWS = 128
BLK = 64
NX, NY, NZ = 4, 4, 8
NPB = NX * NY
SCALE = HD**-0.5 * math.log2(math.e)
LEAST, MOST = 2.0**-80, 2.0**100

PIECE = 16
PARTS = 2 * KVH
WHOLE, FEW, MOST_OF = slice(0, PARTS), slice(0, 3), slice(3, PARTS)
KINDS = {"few": (FEW, 0), "own": (MOST_OF, 0), "other": (MOST_OF, 1)}
ALL, LOW, HIGH = (0, ROWS), (0, ROWS // 2), (ROWS // 2, ROWS // 2)
NEAR, FAR = (0, 5 * PIECE), (5 * PIECE, 3 * PIECE)
N_MSG = 80
N_PASS = 8


def positions(order_ref, block, along, shape):
    index = lax.broadcasted_iota(jnp.int32, shape, along)
    first, second = order_ref[2 * block], order_ref[2 * block + 1]
    return jnp.where(index < BLK, first * BLK + index, second * BLK + index - BLK)


def row_scale(order_ref, len_ref, tags_ref, weight_ref, seq):
    shape = (1, ROWS)
    query_pos = positions(order_ref, seq, 1, shape)
    picked = []
    for k in range(2):
        value = jnp.float32(0.0)
        for v in range(weight_ref.shape[0]):
            value = jnp.where(tags_ref[0, k] == v, weight_ref[v], value)
        picked.append(value)
    index = lax.broadcasted_iota(jnp.int32, shape, 1)
    weight = jnp.where(index < BLK, picked[0], picked[1])
    return jnp.where(query_pos < len_ref[0], weight, 0.0)


def block_bias(order_ref, len_ref, seq, block):
    shape = (ROWS, ROWS)
    query_pos = positions(order_ref, seq, 1, shape)
    key_pos = positions(order_ref, block, 0, shape)
    allowed = (key_pos <= query_pos) & (key_pos < len_ref[0])
    return jnp.where(allowed, 0.0, -jnp.inf).astype(F32)


def gather_attend(
    len_in, order_in, tags_in, weight_in, q_in, own_in, piece_in,
    out_hbm, bad_ref, kept_ref,
    len_ref, order_ref, tags_ref, weight_ref, q_ref,
    out_ref, kv, qa, acc, bias, load_sem, send_sem, recv_sem, keep_sem,
):
    grp, smp, seq = lax.axis_index("grp"), lax.axis_index("smp"), lax.axis_index("seq")
    x_hi, z = lax.div(seq, NZ), lax.rem(seq, NZ)
    x_lo, y = lax.div(smp, NY), lax.rem(smp, NY)
    x = x_hi * 2 + x_lo

    def device(dx, dy, dz):
        xx, yy, zz = lax.rem(x + dx + NX, NX), lax.rem(y + dy + NY, NY), lax.rem(z + dz + NZ, NZ)
        return (grp, lax.rem(xx, 2) * NY + yy, lax.div(xx, 2) * NZ + zz)

    def rblock(lane, dz):
        column = x_hi if lane == 0 else 1 - x_hi
        return NPB + column * NZ + lax.rem(z + dz + NZ, NZ)

    def pblock(dx, dy):
        return lax.rem(x + dx + NX, NX) * NY + lax.rem(y + dy + NY, NY)

    peers = [device(0, 0, d) for d in range(1, NZ)]
    peers += [device(d, 0, 0) for d in range(1, NX)] + [device(0, 1, 0), device(0, -1, 0)]
    barrier = pltpu.get_barrier_semaphore()
    for peer in peers:
        pl.semaphore_signal(barrier, inc=1, device_id=peer, device_id_type=MESH)

    own_block, own_prompt = rblock(0, 0), pblock(0, 0)
    pairs = [(piece_in.at[:, k * HD : (k + 1) * HD], kv.at[k, own_prompt, 0:PIECE, :]) for k in range(PARTS)]
    pairs += [(own_in.at[:, k * HD : (k + 1) * HD], kv.at[k, own_block]) for k in range(PARTS)]
    pairs += [(q_in, q_ref), (len_in, len_ref), (order_in, order_ref), (tags_in, tags_ref), (weight_in, weight_ref)]
    loads = [pltpu.make_async_copy(src, dst, load_sem.at[i]) for i, (src, dst) in enumerate(pairs)]
    for load in loads:
        load.start()

    sent = {}
    numbers = {}

    def number(name):
        return numbers.setdefault(name, len(numbers))

    def piece_of(which, block, rows):
        start, size = rows
        return kv.at[which, block, pl.ds(start, size), :]

    def copy(name, ref, to):
        m = number(name)
        return pltpu.make_async_remote_copy(
            src_ref=ref[0], dst_ref=ref[1], send_sem=send_sem.at[m], recv_sem=recv_sem.at[m],
            device_id=to, device_id_type=MESH,
        )

    def send(name, which, block, rows, to, there=None):
        src = piece_of(which, block, rows)
        dst = src if there is None else piece_of(which, block, there)
        sent[name] = (which, rows)
        copy(name, (src, dst), to).start()

    def arrive(name, which, block, rows=ALL):
        here = piece_of(which, block, rows)
        copy(name, (here, here), device(0, 0, 1)).wait_recv()

    def z_step(kind, step):
        which, lane = KINDS[kind]
        low, high = (LOW, HIGH) if step == NZ // 2 else (ALL, ALL)
        send((kind, step, 1), which, rblock(lane, 1 - step), low, device(0, 0, 1))
        send((kind, step, -1), which, rblock(lane, step - 1), high, device(0, 0, -1))

    def z_arrive(kind, step):
        which, lane = KINDS[kind]
        low, high = (LOW, HIGH) if step == NZ // 2 else (ALL, ALL)
        arrive((kind, step, 1), which, rblock(lane, -step), low)
        arrive((kind, step, -1), which, rblock(lane, step), high)

    def x_step(step, rows, tag=0):
        low, high = (LOW, HIGH) if step == 2 else (rows, rows)
        send(("x", step, 1, tag), WHOLE, pblock(1 - step, 0), low, device(1, 0, 0))
        send(("x", step, -1, tag), WHOLE, pblock(step - 1, 0), high, device(-1, 0, 0))

    def x_arrive(step, rows, tag=0):
        low, high = (LOW, HIGH) if step == 2 else (rows, rows)
        arrive(("x", step, 1, tag), WHOLE, pblock(-step, 0), low)
        arrive(("x", step, -1, tag), WHOLE, pblock(step, 0), high)

    def y_step(dx, step, right=ALL, left=ALL, tag=0):
        send(("y", dx, step, 1, tag), WHOLE, pblock(dx, 1 - step), right, device(0, 1, 0))
        send(("y", dx, step, -1, tag), WHOLE, pblock(dx, step - 1), left, device(0, -1, 0))

    def y_arrive(dx, step, right=ALL, left=ALL, tag=0):
        arrive(("y", dx, step, 1, tag), WHOLE, pblock(dx, -step), right)
        arrive(("y", dx, step, -1, tag), WHOLE, pblock(dx, step), left)

    def far_step():
        for d in (1, -1):
            send(("far", d), WHOLE, pblock(0, 2), ALL, device(d, 0, 0))

    def far_arrive():
        for d in (1, -1):
            arrive(("far", d), WHOLE, pblock(-d, 2))

    def cross(step):
        for d in sorted({-step, step} if step < NZ // 2 else {step}):
            send(("cross", d), FEW, rblock(0, d), ALL, device(2, 0, 0))

    def cross_arrive(step):
        for d in sorted({-step, step} if step < NZ // 2 else {step}):
            arrive(("cross", d), FEW, rblock(1, d))

    for load in loads:
        load.wait()
    bias[0] = jnp.zeros((ROWS, ROWS), F32)

    def set_bias(block, _):
        bias[block + 1] = block_bias(order_ref, len_ref, seq, block)
        return 0

    lax.fori_loop(0, 2 * NZ, set_bias, 0)
    acc[...] = jnp.zeros_like(acc)

    pl.semaphore_wait(barrier, len(peers))

    slots = {0: 0, -1: 1, 1: 2, -2: 3, 2: 4, -3: 5, 3: 6, 4: 7}

    def slot(d):
        return (slots[d] * PIECE, PIECE)

    for d in (1, -1, 2, -2, 3, -3, 4):
        send(("piece", d), WHOLE, own_prompt, slot(0), device(0, 0, d), there=slot(-d if d < 4 else 4))
    send("most", MOST_OF, own_block, ALL, device(2, 0, 0))
    cross(0)
    z_step("few", 1)
    z_step("own", 1)

    for h in range(KVH):
        for g in range(GW):
            column = (h * GW + g) * HD
            scaled = q_ref[:, column : column + HD].T.astype(F32) * SCALE
            high = scaled.astype(BF16)
            qa[h, 0:HD, g * ROWS : (g + 1) * ROWS] = high
            qa[h, HD : 2 * HD, g * ROWS : (g + 1) * ROWS] = (scaled - high.astype(F32)).astype(BF16)
    def pieces_arrive(distances):
        for d in distances:
            arrive(("piece", d), WHOLE, own_prompt, slot(-d if d < 4 else 4))

    def event_0():
        pieces_arrive((1, -1, 2, -2))
        y_step(0, 1, NEAR, NEAR)
        x_step(1, NEAR)
        z_arrive("few", 1)
        z_step("few", 2)
        cross(1)
        arrive("most", MOST_OF, rblock(1, 0))
        z_step("other", 1)
        pieces_arrive((3, -3, 4))
        y_step(0, 1, FAR, FAR, 1)
        x_step(1, FAR, 1)

    def event_1():
        x_arrive(1, NEAR)
        y_step(1, 1, NEAR, NEAR)
        y_step(-1, 1, NEAR, NEAR)
        z_arrive("own", 1)
        z_step("own", 2)

    def event_2():
        y_arrive(0, 1, NEAR, NEAR)
        y_arrive(0, 1, FAR, FAR, 1)
        y_step(0, 2, LOW, HIGH)

    def event_3():
        z_arrive("few", 2)
        z_step("few", 3)
        cross(2)
        x_arrive(1, FAR, 1)
        x_step(2, ALL)
        y_step(1, 1, FAR, FAR, 1)
        y_step(-1, 1, FAR, FAR, 1)

    def event_4():
        z_arrive("other", 1)
        z_step("other", 2)
        cross_arrive(1)

    def event_5():
        z_arrive("own", 2)
        z_step("own", 3)

    def event_6():
        z_arrive("few", 3)
        z_step("few", 4)
        cross(3)
        y_arrive(0, 2, LOW, HIGH)
        far_step()
        cross_arrive(0)

    def event_7():
        x_arrive(2, ALL)
        y_step(2, 1, LOW, HIGH)
        y_step(2, 1, HIGH, LOW, 1)
        y_arrive(-1, 1, NEAR, NEAR)
        y_arrive(-1, 1, FAR, FAR, 1)

    def event_8():
        z_arrive("other", 2)
        z_step("other", 3)
        cross_arrive(2)

    def event_9():
        y_arrive(1, 1, NEAR, NEAR)
        y_arrive(1, 1, FAR, FAR, 1)

    def event_10():
        z_arrive("own", 3)
        z_step("own", 4)

    def event_11():
        z_arrive("few", 4)
        cross(4)
        y_arrive(2, 1, LOW, HIGH)
        y_step(2, 2, LOW, HIGH)
        y_arrive(2, 1, HIGH, LOW, 1)

    def event_12():
        z_arrive("other", 3)
        z_step("other", 4)
        cross_arrive(3)

    def event_13():
        far_arrive()

    def event_14():
        y_arrive(2, 2, LOW, HIGH)

    def event_15():
        z_arrive("own", 4)
        z_arrive("other", 4)
        cross_arrive(4)

    units = [
        (event_0, own_block, own_prompt),
        (event_1, rblock(0, -1), rblock(0, 1)),
        (event_2, pblock(0, -1), pblock(0, 1)),
        (event_3, pblock(1, 0), pblock(-1, 0)),
        (event_4, rblock(1, -1), rblock(1, 1)),
        (event_5, rblock(0, -2), rblock(0, 2)),
        (event_6, rblock(1, 0), pblock(0, 2)),
        (event_7, pblock(-1, -1), pblock(-1, 1)),
        (event_8, rblock(1, -2), rblock(1, 2)),
        (event_9, pblock(1, -1), pblock(1, 1)),
        (event_10, rblock(0, -3), rblock(0, 3)),
        (event_11, pblock(2, -1), pblock(2, 1)),
        (event_12, rblock(1, -3), rblock(1, 3)),
        (event_13, pblock(1, 2), pblock(-1, 2)),
        (event_14, pblock(2, 0), pblock(2, 2)),
        (event_15, rblock(0, 4), rblock(1, 4)),
    ]
    ones = jnp.ones((16, 2 * ROWS), BF16)

    def keep(unit, block, which):
        return pltpu.make_async_copy(kv.at[:, block], kept_ref.at[:, block], keep_sem.at[2 * unit + which])

    def pick(t, which):
        block = units[0][which]
        for i, unit in enumerate(units):
            block = jnp.where(t == i, unit[which], block)
        return block

    def work(t, _):
        for i, unit in enumerate(units):
            pl.when(t == i)(unit[0])
        one, two = pick(t, 1), pick(t, 2)
        keep(t, one, 0).start()
        keep(t, two, 1).start()
        bias_one = bias.at[jnp.maximum(one - (NPB - 1), 0)]
        bias_two = bias.at[jnp.maximum(two - (NPB - 1), 0)]

        def scores(h):
            k = jnp.concatenate([kv[h, one], kv[h, two]], axis=0)
            return jnp.dot(jnp.concatenate([k, k], axis=1), qa[h], preferred_element_type=F32)

        def weights(s):
            b = jnp.concatenate([bias_one[...], bias_two[...]], axis=0)
            s = jnp.concatenate([s[:, g * ROWS : (g + 1) * ROWS] + b for g in range(GW)], axis=1)
            return jnp.exp2(s).astype(BF16)

        def mix(h, p):
            v = jnp.concatenate([kv[KVH + h, one].T, kv[KVH + h, two].T], axis=1)
            acc[h] += jnp.dot(jnp.concatenate([v, ones], axis=0), p, preferred_element_type=F32)

        s, p = {0: scores(0)}, {}
        for h in range(KVH + 1):
            if h + 1 < KVH:
                s[h + 1] = scores(h + 1)
            if h >= 1:
                mix(h - 1, p.pop(h - 1))
            if h < KVH:
                p[h] = weights(s.pop(h))
        return 0

    lax.fori_loop(0, len(units), work, 0)

    scale_row = row_scale(order_ref, len_ref, tags_ref, weight_ref, seq)
    bad = jnp.zeros((1, ROWS), F32)
    spans = [slice(h * GW * HD, (h + 1) * GW * HD) for h in range(KVH)]
    stores = [pltpu.make_async_copy(out_ref.at[:, c], out_hbm.at[:, c], load_sem.at[i]) for i, c in enumerate(spans)]
    for h in range(KVH):
        for g in range(GW):
            columns = slice(g * ROWS, (g + 1) * ROWS)
            total = acc[h, HD : HD + 1, columns]
            bad = jnp.where((total >= LEAST) & (total <= MOST), bad, 1.0)
            mixed = (acc[h, 0:HD, columns] * (scale_row / total)).astype(BF16)
            column = (h * GW + g) * HD
            out_ref[:, column : column + HD] = mixed.T
        stores[h].start()
    bad_ref[...] = bad

    for store in stores:
        store.wait()
    for t, unit in enumerate(units):
        keep(t, unit[1], 0).wait()
        keep(t, unit[2], 1).wait()
    for name, (which, rows) in sent.items():
        here = piece_of(which, own_block, rows)
        copy(name, (here, here), device(0, 0, 1)).wait_send()


def check_rows(
    len_in, order_in, tags_in, weight_in, bad_in, q_ref, kept_ref, first_ref,
    out_ref,
    len_ref, order_ref, tags_ref, weight_ref, bad_ref, q, kv, out, sem, pass_sem,
):
    seq = lax.axis_index("seq")
    parts = [slice(i * ROWS // N_PASS, (i + 1) * ROWS // N_PASS) for i in range(N_PASS)]
    into = [pltpu.make_async_copy(first_ref.at[p], out.at[p], pass_sem.at[0, i]) for i, p in enumerate(parts)]
    onto = [pltpu.make_async_copy(out.at[p], out_ref.at[p], pass_sem.at[1, i]) for i, p in enumerate(parts)]
    flag = pltpu.make_async_copy(bad_in, bad_ref, sem)
    for load in into:
        load.start()
    flag.start()
    for load, store in zip(into, onto):
        load.wait()
        store.start()
    flag.wait()
    bad = jnp.max(bad_ref[...])
    for store in onto:
        store.wait()

    @pl.when(bad > 0.0)
    def redo():
        scalars = ((len_in, len_ref), (order_in, order_ref), (tags_in, tags_ref), (weight_in, weight_ref))
        for src, dst in ((q_ref, q), (kept_ref, kv), *scalars):
            fetch = pltpu.make_async_copy(src, dst, sem)
            fetch.start()
            fetch.wait()
        scale_row = row_scale(order_ref, len_ref, tags_ref, weight_ref, seq)

        def head(index, _):
            columns = pl.ds(pl.multiple_of(index * HD, HD), HD)
            kv_head = lax.div(index, GW)
            queries = q[:, columns]

            def scores(block):
                s = lax.dot_general(
                    kv[kv_head, block], queries, (((1,), (1,)), ((), ())), preferred_element_type=F32
                )
                b = block_bias(order_ref, len_ref, seq, jnp.maximum(block - NPB, 0))
                return jnp.where(block < NPB, s * SCALE, s * SCALE + b)

            def top_of(block, top):
                return jnp.maximum(top, jnp.max(scores(block), axis=0, keepdims=True))

            blocks = kv.shape[1]
            top = lax.fori_loop(0, blocks, top_of, jnp.full((1, ROWS), -jnp.inf, F32))

            def add(block, carry):
                total, mixed = carry
                w = jnp.exp2(scores(block) - top)
                total += jnp.sum(w, axis=0, keepdims=True)
                mixed += jnp.dot(kv[KVH + kv_head, block].T, w.astype(BF16), preferred_element_type=F32)
                return total, mixed

            total, mixed = lax.fori_loop(
                0, blocks, add, (jnp.zeros((1, ROWS), F32), jnp.zeros((HD, ROWS), F32))
            )
            out[:, columns] = (mixed * (scale_row / total)).astype(BF16).T
            return 0

        lax.fori_loop(0, H, head, 0)
        store = pltpu.make_async_copy(out, out_ref, sem)
        store.start()
        store.wait()


def shards(resp_q, resp_kv, prompt_kv, resp_len, block_order, tags, ver_weight):
    blocks = NPB + 2 * NZ
    vmem = pl.BlockSpec(memory_space=pltpu.VMEM)
    hbm = pl.BlockSpec(memory_space=pltpu.HBM)
    scalars = (resp_len, block_order, tags, ver_weight)
    queries = resp_q[0]
    kv_shape = (PARTS, blocks, ROWS, HD)
    keys = blocks * ROWS
    attended, bad, kept = pl.pallas_call(
        gather_attend,
        out_shape=(
            jax.ShapeDtypeStruct((ROWS, H * HD), BF16),
            jax.ShapeDtypeStruct((1, ROWS), F32),
            jax.ShapeDtypeStruct(kv_shape, BF16),
        ),
        in_specs=[hbm] * 7,
        out_specs=(hbm, vmem, hbm),
        scratch_shapes=[pltpu.SMEM(a.shape, a.dtype) for a in scalars]
        + [
            pltpu.VMEM((ROWS, H * HD), BF16),
            pltpu.VMEM((ROWS, H * HD), BF16),
            pltpu.VMEM(kv_shape, BF16),
            pltpu.VMEM((KVH, 2 * HD, GW * ROWS), BF16),
            pltpu.VMEM((KVH, HD + 16, GW * ROWS), F32),
            pltpu.VMEM((2 * NZ + 1, ROWS, ROWS), F32),
            pltpu.SemaphoreType.DMA((2 * PARTS + 5,)),
            pltpu.SemaphoreType.DMA((N_MSG,)),
            pltpu.SemaphoreType.DMA((N_MSG,)),
            pltpu.SemaphoreType.DMA((blocks,)),
        ],
        compiler_params=pltpu.CompilerParams(
            collective_id=0, has_side_effects=True, vmem_limit_bytes=60 * 2**20
        ),
        cost_estimate=pl.CostEstimate(
            flops=4 * ROWS * H * HD * keys, bytes_accessed=4 * keys * HALF, transcendentals=ROWS * H * keys
        ),
    )(*scalars, queries, resp_kv[0], prompt_kv)
    final = pl.pallas_call(
        check_rows,
        out_shape=jax.ShapeDtypeStruct((ROWS, H * HD), BF16),
        in_specs=[hbm] * 8,
        out_specs=hbm,
        scratch_shapes=[pltpu.SMEM(a.shape, a.dtype) for a in scalars]
        + [
            pltpu.VMEM((1, ROWS), F32),
            pltpu.VMEM((ROWS, H * HD), BF16),
            pltpu.VMEM(kv_shape, BF16),
            pltpu.VMEM((ROWS, H * HD), BF16),
            pltpu.SemaphoreType.DMA,
            pltpu.SemaphoreType.DMA((2, N_PASS)),
        ],
        compiler_params=pltpu.CompilerParams(vmem_limit_bytes=60 * 2**20),
    )(*scalars, bad, queries, kept, attended)
    return final[None]


def solution(mesh):
    in_specs = (
        P(("grp", "smp"), "seq", None),
        P(("grp", "smp"), "seq", None),
        P(("grp", "smp", "seq"), None),
        P(("grp", "smp")),
        P("grp"),
        P(("grp", "smp"), "seq"),
        P(),
    )
    out_specs = P(("grp", "smp"), "seq", None)
    return jax.shard_map(shards, mesh=mesh, in_specs=in_specs, out_specs=out_specs, check_vma=False)
```

```python
import functools
import math

import jax
import jax.numpy as jnp
from jax import lax
from jax.experimental import pallas as pl
from jax.experimental.pallas import tpu as pltpu
from jax.sharding import PartitionSpec as P

MESH = pl.DeviceIdType.MESH
F32 = jnp.float32
BF16 = jnp.bfloat16
H = 32
KVH = 4
HD = 128
GW = H // KVH
HALF = KVH * HD
ROWS = 128
BLK = 64
NX, NY, NZ = 4, 4, 8
NPB = NX * NY
SCALE = HD**-0.5 * math.log2(math.e)
LEAST, MOST = 2.0**-80, 2.0**100

PIECE = 16
PARTS = 2 * KVH
WHOLE, FEW, MOST_OF = slice(0, PARTS), slice(0, 3), slice(3, PARTS)
KINDS = {"few": (FEW, 0), "own": (MOST_OF, 0), "other": (MOST_OF, 1)}
ALL, LOW, HIGH = (0, ROWS), (0, ROWS // 2), (ROWS // 2, ROWS // 2)
NEAR, FAR = (0, 5 * PIECE), (5 * PIECE, 3 * PIECE)
N_MSG = 80
N_PASS = 8


def positions(order_ref, block, along, shape):
    index = lax.broadcasted_iota(jnp.int32, shape, along)
    first, second = order_ref[2 * block], order_ref[2 * block + 1]
    return jnp.where(index < BLK, first * BLK + index, second * BLK + index - BLK)


def row_scale(order_ref, len_ref, tags_ref, weight_ref, seq):
    shape = (1, ROWS)
    query_pos = positions(order_ref, seq, 1, shape)
    picked = []
    for k in range(2):
        value = jnp.float32(0.0)
        for v in range(weight_ref.shape[0]):
            value = jnp.where(tags_ref[0, k] == v, weight_ref[v], value)
        picked.append(value)
    index = lax.broadcasted_iota(jnp.int32, shape, 1)
    weight = jnp.where(index < BLK, picked[0], picked[1])
    return jnp.where(query_pos < len_ref[0], weight, 0.0)


def block_bias(order_ref, len_ref, seq, block):
    shape = (ROWS, ROWS)
    query_pos = positions(order_ref, seq, 1, shape)
    key_pos = positions(order_ref, block, 0, shape)
    allowed = (key_pos <= query_pos) & (key_pos < len_ref[0])
    return jnp.where(allowed, 0.0, -jnp.inf).astype(F32)


def gather_attend(
    len_in, order_in, tags_in, weight_in, q_in, own_in, piece_in,
    out_hbm, bad_ref, kept_ref,
    len_ref, order_ref, tags_ref, weight_ref, q_ref,
    out_ref, kv, qa, acc, bias, load_sem, send_sem, recv_sem, keep_sem,
):
    grp, smp, seq = lax.axis_index("grp"), lax.axis_index("smp"), lax.axis_index("seq")
    x_hi, z = lax.div(seq, NZ), lax.rem(seq, NZ)
    x_lo, y = lax.div(smp, NY), lax.rem(smp, NY)
    x = x_hi * 2 + x_lo

    def device(dx, dy, dz):
        xx, yy, zz = lax.rem(x + dx + NX, NX), lax.rem(y + dy + NY, NY), lax.rem(z + dz + NZ, NZ)
        return (grp, lax.rem(xx, 2) * NY + yy, lax.div(xx, 2) * NZ + zz)

    def rblock(lane, dz):
        column = x_hi if lane == 0 else 1 - x_hi
        return NPB + column * NZ + lax.rem(z + dz + NZ, NZ)

    def pblock(dx, dy):
        return lax.rem(x + dx + NX, NX) * NY + lax.rem(y + dy + NY, NY)

    peers = [device(0, 0, d) for d in range(1, NZ)]
    peers += [device(d, 0, 0) for d in range(1, NX)] + [device(0, 1, 0), device(0, -1, 0)]
    barrier = pltpu.get_barrier_semaphore()
    for peer in peers:
        pl.semaphore_signal(barrier, inc=1, device_id=peer, device_id_type=MESH)

    own_block, own_prompt = rblock(0, 0), pblock(0, 0)
    pairs = [(piece_in.at[:, k * HD : (k + 1) * HD], kv.at[k, own_prompt, 0:PIECE, :]) for k in range(PARTS)]
    pairs += [(own_in.at[:, k * HD : (k + 1) * HD], kv.at[k, own_block]) for k in range(PARTS)]
    pairs += [(q_in, q_ref), (len_in, len_ref), (order_in, order_ref), (tags_in, tags_ref), (weight_in, weight_ref)]
    loads = [pltpu.make_async_copy(src, dst, load_sem.at[i]) for i, (src, dst) in enumerate(pairs)]
    for load in loads:
        load.start()

    sent = {}
    numbers = {}

    def number(name):
        return numbers.setdefault(name, len(numbers))

    def piece_of(which, block, rows):
        start, size = rows
        return kv.at[which, block, pl.ds(start, size), :]

    def copy(name, ref, to):
        m = number(name)
        return pltpu.make_async_remote_copy(
            src_ref=ref[0], dst_ref=ref[1], send_sem=send_sem.at[m], recv_sem=recv_sem.at[m],
            device_id=to, device_id_type=MESH,
        )

    def send(name, which, block, rows, to, there=None):
        src = piece_of(which, block, rows)
        dst = src if there is None else piece_of(which, block, there)
        sent[name] = (which, rows)
        copy(name, (src, dst), to).start()

    def arrive(name, which, block, rows=ALL):
        here = piece_of(which, block, rows)
        copy(name, (here, here), device(0, 0, 1)).wait_recv()

    def z_step(kind, step):
        which, lane = KINDS[kind]
        low, high = (LOW, HIGH) if step == NZ // 2 else (ALL, ALL)
        send((kind, step, 1), which, rblock(lane, 1 - step), low, device(0, 0, 1))
        send((kind, step, -1), which, rblock(lane, step - 1), high, device(0, 0, -1))

    def z_arrive(kind, step):
        which, lane = KINDS[kind]
        low, high = (LOW, HIGH) if step == NZ // 2 else (ALL, ALL)
        arrive((kind, step, 1), which, rblock(lane, -step), low)
        arrive((kind, step, -1), which, rblock(lane, step), high)

    def x_step(step, rows, tag=0):
        low, high = (LOW, HIGH) if step == 2 else (rows, rows)
        send(("x", step, 1, tag), WHOLE, pblock(1 - step, 0), low, device(1, 0, 0))
        send(("x", step, -1, tag), WHOLE, pblock(step - 1, 0), high, device(-1, 0, 0))

    def x_arrive(step, rows, tag=0):
        low, high = (LOW, HIGH) if step == 2 else (rows, rows)
        arrive(("x", step, 1, tag), WHOLE, pblock(-step, 0), low)
        arrive(("x", step, -1, tag), WHOLE, pblock(step, 0), high)

    def y_step(dx, step, right=ALL, left=ALL, tag=0):
        send(("y", dx, step, 1, tag), WHOLE, pblock(dx, 1 - step), right, device(0, 1, 0))
        send(("y", dx, step, -1, tag), WHOLE, pblock(dx, step - 1), left, device(0, -1, 0))

    def y_arrive(dx, step, right=ALL, left=ALL, tag=0):
        arrive(("y", dx, step, 1, tag), WHOLE, pblock(dx, -step), right)
        arrive(("y", dx, step, -1, tag), WHOLE, pblock(dx, step), left)

    def far_step():
        for d in (1, -1):
            send(("far", d), WHOLE, pblock(0, 2), ALL, device(d, 0, 0))

    def far_arrive():
        for d in (1, -1):
            arrive(("far", d), WHOLE, pblock(-d, 2))

    def cross(step):
        for d in sorted({-step, step} if step < NZ // 2 else {step}):
            send(("cross", d), FEW, rblock(0, d), ALL, device(2, 0, 0))

    def cross_arrive(step):
        for d in sorted({-step, step} if step < NZ // 2 else {step}):
            arrive(("cross", d), FEW, rblock(1, d))

    for load in loads:
        load.wait()
    bias[0] = jnp.zeros((ROWS, ROWS), F32)

    def set_bias(block, _):
        bias[block + 1] = block_bias(order_ref, len_ref, seq, block)
        return 0

    lax.fori_loop(0, 2 * NZ, set_bias, 0)
    acc[...] = jnp.zeros_like(acc)

    pl.semaphore_wait(barrier, len(peers))

    slots = {0: 0, -1: 1, 1: 2, -2: 3, 2: 4, -3: 5, 3: 6, 4: 7}

    def slot(d):
        return (slots[d] * PIECE, PIECE)

    for d in (1, -1, 2, -2, 3, -3, 4):
        send(("piece", d), WHOLE, own_prompt, slot(0), device(0, 0, d), there=slot(-d if d < 4 else 4))
    send("most", MOST_OF, own_block, ALL, device(2, 0, 0))
    cross(0)
    z_step("few", 1)
    z_step("own", 1)

    for h in range(KVH):
        for g in range(GW):
            column = (h * GW + g) * HD
            scaled = q_ref[:, column : column + HD].T.astype(F32) * SCALE
            high = scaled.astype(BF16)
            qa[h, 0:HD, g * ROWS : (g + 1) * ROWS] = high
            qa[h, HD : 2 * HD, g * ROWS : (g + 1) * ROWS] = (scaled - high.astype(F32)).astype(BF16)
    def pieces_arrive(distances):
        for d in distances:
            arrive(("piece", d), WHOLE, own_prompt, slot(-d if d < 4 else 4))

    def event_0():
        pieces_arrive((1, -1, 2, -2))
        y_step(0, 1, NEAR, NEAR)
        x_step(1, NEAR)
        z_arrive("few", 1)
        z_step("few", 2)
        cross(1)
        arrive("most", MOST_OF, rblock(1, 0))
        z_step("other", 1)
        pieces_arrive((3, -3, 4))
        y_step(0, 1, FAR, FAR, 1)
        x_step(1, FAR, 1)

    def event_1():
        x_arrive(1, NEAR)
        y_step(1, 1, NEAR, NEAR)
        y_step(-1, 1, NEAR, NEAR)
        z_arrive("own", 1)
        z_step("own", 2)

    def event_2():
        y_arrive(0, 1, NEAR, NEAR)
        y_arrive(0, 1, FAR, FAR, 1)
        y_step(0, 2, LOW, HIGH)

    def event_3():
        z_arrive("few", 2)
        z_step("few", 3)
        cross(2)
        x_arrive(1, FAR, 1)
        x_step(2, ALL)
        y_step(1, 1, FAR, FAR, 1)
        y_step(-1, 1, FAR, FAR, 1)

    def event_4():
        z_arrive("other", 1)
        z_step("other", 2)
        cross_arrive(1)

    def event_5():
        z_arrive("own", 2)
        z_step("own", 3)

    def event_6():
        z_arrive("few", 3)
        z_step("few", 4)
        cross(3)
        y_arrive(0, 2, LOW, HIGH)
        far_step()
        cross_arrive(0)

    def event_7():
        x_arrive(2, ALL)
        y_step(2, 1, LOW, HIGH)
        y_step(2, 1, HIGH, LOW, 1)
        y_arrive(-1, 1, NEAR, NEAR)
        y_arrive(-1, 1, FAR, FAR, 1)

    def event_8():
        z_arrive("other", 2)
        z_step("other", 3)
        cross_arrive(2)

    def event_9():
        y_arrive(1, 1, NEAR, NEAR)
        y_arrive(1, 1, FAR, FAR, 1)

    def event_10():
        z_arrive("own", 3)
        z_step("own", 4)

    def event_11():
        z_arrive("few", 4)
        cross(4)
        y_arrive(2, 1, LOW, HIGH)
        y_step(2, 2, LOW, HIGH)
        y_arrive(2, 1, HIGH, LOW, 1)

    def event_12():
        z_arrive("other", 3)
        z_step("other", 4)
        cross_arrive(3)

    def event_13():
        far_arrive()

    def event_14():
        y_arrive(2, 2, LOW, HIGH)

    def event_15():
        z_arrive("own", 4)
        z_arrive("other", 4)
        cross_arrive(4)

    units = [
        (event_0, own_block, own_prompt),
        (event_1, rblock(0, -1), rblock(0, 1)),
        (event_2, pblock(0, -1), pblock(0, 1)),
        (event_3, pblock(1, 0), pblock(-1, 0)),
        (event_4, rblock(1, -1), rblock(1, 1)),
        (event_5, rblock(0, -2), rblock(0, 2)),
        (event_6, rblock(1, 0), pblock(0, 2)),
        (event_7, pblock(-1, -1), pblock(-1, 1)),
        (event_8, rblock(1, -2), rblock(1, 2)),
        (event_9, pblock(1, -1), pblock(1, 1)),
        (event_10, rblock(0, -3), rblock(0, 3)),
        (event_11, pblock(2, -1), pblock(2, 1)),
        (event_12, rblock(1, -3), rblock(1, 3)),
        (event_13, pblock(1, 2), pblock(-1, 2)),
        (event_14, pblock(2, 0), pblock(2, 2)),
        (event_15, rblock(0, 4), rblock(1, 4)),
    ]
    ones = jnp.ones((16, 2 * ROWS), BF16)

    def keep(unit, block, which):
        return pltpu.make_async_copy(kv.at[:, block], kept_ref.at[:, block], keep_sem.at[2 * unit + which])

    def pick(t, which):
        block = units[0][which]
        for i, unit in enumerate(units):
            block = jnp.where(t == i, unit[which], block)
        return block

    def work(t, one, two, finish=None):
        keep(t, one, 0).start()
        keep(t, two, 1).start()
        bias_one = bias.at[jnp.maximum(one - (NPB - 1), 0)]
        bias_two = bias.at[jnp.maximum(two - (NPB - 1), 0)]

        def scores(h):
            k = jnp.concatenate([kv[h, one], kv[h, two]], axis=0)
            return jnp.dot(jnp.concatenate([k, k], axis=1), qa[h], preferred_element_type=F32)

        def weights(s):
            b = jnp.concatenate([bias_one[...], bias_two[...]], axis=0)
            s = jnp.concatenate([s[:, g * ROWS : (g + 1) * ROWS] + b for g in range(GW)], axis=1)
            return jnp.exp2(s).astype(BF16)

        def mix(h, p):
            v = jnp.concatenate([kv[KVH + h, one].T, kv[KVH + h, two].T], axis=1)
            acc[h] += jnp.dot(jnp.concatenate([v, ones], axis=0), p, preferred_element_type=F32)

        s, p = {0: scores(0)}, {}
        for h in range(KVH + 1):
            if h + 1 < KVH:
                s[h + 1] = scores(h + 1)
            if h >= 1:
                mix(h - 1, p.pop(h - 1))
                if finish is not None:
                    finish(h - 1)
            if h < KVH:
                p[h] = weights(s.pop(h))

    def step(t, _):
        for i, unit in enumerate(units[:-1]):
            pl.when(t == i)(unit[0])
        work(t, pick(t, 1), pick(t, 2))
        return 0

    lax.fori_loop(0, len(units) - 1, step, 0)

    scale_row = row_scale(order_ref, len_ref, tags_ref, weight_ref, seq)
    spans = [slice(h * GW * HD, (h + 1) * GW * HD) for h in range(KVH)]
    stores = [pltpu.make_async_copy(out_ref.at[:, c], out_hbm.at[:, c], load_sem.at[i]) for i, c in enumerate(spans)]
    bad_ref[...] = jnp.zeros((1, ROWS), F32)

    def finish(h):
        bad = bad_ref[...]
        for g in range(GW):
            columns = slice(g * ROWS, (g + 1) * ROWS)
            total = acc[h, HD : HD + 1, columns]
            bad = jnp.where((total >= LEAST) & (total <= MOST), bad, 1.0)
            mixed = (acc[h, 0:HD, columns] * (scale_row / total)).astype(BF16)
            column = (h * GW + g) * HD
            out_ref[:, column : column + HD] = mixed.T
        bad_ref[...] = bad
        stores[h].start()

    last = len(units) - 1
    units[last][0]()
    work(last, units[last][1], units[last][2], finish)

    for store in stores:
        store.wait()
    for t, unit in enumerate(units):
        keep(t, unit[1], 0).wait()
        keep(t, unit[2], 1).wait()
    for name, (which, rows) in sent.items():
        here = piece_of(which, own_block, rows)
        copy(name, (here, here), device(0, 0, 1)).wait_send()


def check_rows(
    len_in, order_in, tags_in, weight_in, bad_in, q_ref, kept_ref, first_ref,
    out_ref,
    len_ref, order_ref, tags_ref, weight_ref, bad_ref, q, kv, out, sem, pass_sem,
):
    seq = lax.axis_index("seq")
    parts = [slice(i * ROWS // N_PASS, (i + 1) * ROWS // N_PASS) for i in range(N_PASS)]
    into = [pltpu.make_async_copy(first_ref.at[p], out.at[p], pass_sem.at[0, i]) for i, p in enumerate(parts)]
    onto = [pltpu.make_async_copy(out.at[p], out_ref.at[p], pass_sem.at[1, i]) for i, p in enumerate(parts)]
    flag = pltpu.make_async_copy(bad_in, bad_ref, sem)
    for load in into:
        load.start()
    flag.start()
    for load, store in zip(into, onto):
        load.wait()
        store.start()
    flag.wait()
    bad = jnp.max(bad_ref[...])
    for store in onto:
        store.wait()

    @pl.when(bad > 0.0)
    def redo():
        scalars = ((len_in, len_ref), (order_in, order_ref), (tags_in, tags_ref), (weight_in, weight_ref))
        for src, dst in ((q_ref, q), (kept_ref, kv), *scalars):
            fetch = pltpu.make_async_copy(src, dst, sem)
            fetch.start()
            fetch.wait()
        scale_row = row_scale(order_ref, len_ref, tags_ref, weight_ref, seq)

        def head(index, _):
            columns = pl.ds(pl.multiple_of(index * HD, HD), HD)
            kv_head = lax.div(index, GW)
            queries = q[:, columns]

            def scores(block):
                s = lax.dot_general(
                    kv[kv_head, block], queries, (((1,), (1,)), ((), ())), preferred_element_type=F32
                )
                b = block_bias(order_ref, len_ref, seq, jnp.maximum(block - NPB, 0))
                return jnp.where(block < NPB, s * SCALE, s * SCALE + b)

            def top_of(block, top):
                return jnp.maximum(top, jnp.max(scores(block), axis=0, keepdims=True))

            blocks = kv.shape[1]
            top = lax.fori_loop(0, blocks, top_of, jnp.full((1, ROWS), -jnp.inf, F32))

            def add(block, carry):
                total, mixed = carry
                w = jnp.exp2(scores(block) - top)
                total += jnp.sum(w, axis=0, keepdims=True)
                mixed += jnp.dot(kv[KVH + kv_head, block].T, w.astype(BF16), preferred_element_type=F32)
                return total, mixed

            total, mixed = lax.fori_loop(
                0, blocks, add, (jnp.zeros((1, ROWS), F32), jnp.zeros((HD, ROWS), F32))
            )
            out[:, columns] = (mixed * (scale_row / total)).astype(BF16).T
            return 0

        lax.fori_loop(0, H, head, 0)
        store = pltpu.make_async_copy(out, out_ref, sem)
        store.start()
        store.wait()


def shards(resp_q, resp_kv, prompt_kv, resp_len, block_order, tags, ver_weight):
    blocks = NPB + 2 * NZ
    vmem = pl.BlockSpec(memory_space=pltpu.VMEM)
    hbm = pl.BlockSpec(memory_space=pltpu.HBM)
    scalars = (resp_len, block_order, tags, ver_weight)
    queries = resp_q[0]
    kv_shape = (PARTS, blocks, ROWS, HD)
    keys = blocks * ROWS
    attended, bad, kept = pl.pallas_call(
        gather_attend,
        out_shape=(
            jax.ShapeDtypeStruct((ROWS, H * HD), BF16),
            jax.ShapeDtypeStruct((1, ROWS), F32),
            jax.ShapeDtypeStruct(kv_shape, BF16),
        ),
        in_specs=[hbm] * 7,
        out_specs=(hbm, vmem, hbm),
        scratch_shapes=[pltpu.SMEM(a.shape, a.dtype) for a in scalars]
        + [
            pltpu.VMEM((ROWS, H * HD), BF16),
            pltpu.VMEM((ROWS, H * HD), BF16),
            pltpu.VMEM(kv_shape, BF16),
            pltpu.VMEM((KVH, 2 * HD, GW * ROWS), BF16),
            pltpu.VMEM((KVH, HD + 16, GW * ROWS), F32),
            pltpu.VMEM((2 * NZ + 1, ROWS, ROWS), F32),
            pltpu.SemaphoreType.DMA((2 * PARTS + 5,)),
            pltpu.SemaphoreType.DMA((N_MSG,)),
            pltpu.SemaphoreType.DMA((N_MSG,)),
            pltpu.SemaphoreType.DMA((blocks,)),
        ],
        compiler_params=pltpu.CompilerParams(
            collective_id=0, has_side_effects=True, vmem_limit_bytes=60 * 2**20
        ),
        cost_estimate=pl.CostEstimate(
            flops=4 * ROWS * H * HD * keys, bytes_accessed=4 * keys * HALF, transcendentals=ROWS * H * keys
        ),
    )(*scalars, queries, resp_kv[0], prompt_kv)
    final = pl.pallas_call(
        check_rows,
        out_shape=jax.ShapeDtypeStruct((ROWS, H * HD), BF16),
        in_specs=[hbm] * 8,
        out_specs=hbm,
        scratch_shapes=[pltpu.SMEM(a.shape, a.dtype) for a in scalars]
        + [
            pltpu.VMEM((1, ROWS), F32),
            pltpu.VMEM((ROWS, H * HD), BF16),
            pltpu.VMEM(kv_shape, BF16),
            pltpu.VMEM((ROWS, H * HD), BF16),
            pltpu.SemaphoreType.DMA,
            pltpu.SemaphoreType.DMA((2, N_PASS)),
        ],
        compiler_params=pltpu.CompilerParams(vmem_limit_bytes=60 * 2**20),
    )(*scalars, bad, queries, kept, attended)
    return final[None]


def solution(mesh):
    in_specs = (
        P(("grp", "smp"), "seq", None),
        P(("grp", "smp"), "seq", None),
        P(("grp", "smp", "seq"), None),
        P(("grp", "smp")),
        P("grp"),
        P(("grp", "smp"), "seq"),
        P(),
    )
    out_specs = P(("grp", "smp"), "seq", None)
    return jax.shard_map(shards, mesh=mesh, in_specs=in_specs, out_specs=out_specs, check_vma=False)
```

```python
import functools
import math

import jax
import jax.numpy as jnp
from jax import lax
from jax.experimental import pallas as pl
from jax.experimental.pallas import tpu as pltpu
from jax.sharding import PartitionSpec as P

MESH = pl.DeviceIdType.MESH
F32 = jnp.float32
BF16 = jnp.bfloat16
H = 32
KVH = 4
HD = 128
GW = H // KVH
HALF = KVH * HD
ROWS = 128
BLK = 64
NX, NY, NZ = 4, 4, 8
NPB = NX * NY
SCALE = HD**-0.5 * math.log2(math.e)
LEAST, MOST = 2.0**-80, 2.0**100

PIECE = 16
PARTS = 2 * KVH
WHOLE, FEW, MOST_OF = slice(0, PARTS), slice(0, 3), slice(3, PARTS)
KINDS = {"few": (FEW, 0), "own": (MOST_OF, 0), "other": (MOST_OF, 1)}
ALL, LOW, HIGH = (0, ROWS), (0, ROWS // 2), (ROWS // 2, ROWS // 2)
NEAR, FAR = (0, 5 * PIECE), (5 * PIECE, 3 * PIECE)
N_MSG = 80
N_PASS = 8


def positions(order_ref, block, along, shape):
    index = lax.broadcasted_iota(jnp.int32, shape, along)
    first, second = order_ref[2 * block], order_ref[2 * block + 1]
    return jnp.where(index < BLK, first * BLK + index, second * BLK + index - BLK)


def row_scale(order_ref, len_ref, tags_ref, weight_ref, seq):
    shape = (1, ROWS)
    query_pos = positions(order_ref, seq, 1, shape)
    picked = []
    for k in range(2):
        value = jnp.float32(0.0)
        for v in range(weight_ref.shape[0]):
            value = jnp.where(tags_ref[0, k] == v, weight_ref[v], value)
        picked.append(value)
    index = lax.broadcasted_iota(jnp.int32, shape, 1)
    weight = jnp.where(index < BLK, picked[0], picked[1])
    return jnp.where(query_pos < len_ref[0], weight, 0.0)


def block_bias(order_ref, len_ref, seq, block):
    shape = (ROWS, ROWS)
    query_pos = positions(order_ref, seq, 1, shape)
    key_pos = positions(order_ref, block, 0, shape)
    allowed = (key_pos <= query_pos) & (key_pos < len_ref[0])
    return jnp.where(allowed, 0.0, -jnp.inf).astype(F32)


def gather_attend(
    len_in, order_in, tags_in, weight_in, q_in, own_in, piece_in,
    out_hbm, bad_ref, kept_ref,
    len_ref, order_ref, tags_ref, weight_ref, q_ref,
    out_ref, kv, qa, acc, bias, load_sem, send_sem, recv_sem, keep_sem,
):
    grp, smp, seq = lax.axis_index("grp"), lax.axis_index("smp"), lax.axis_index("seq")
    x_hi, z = lax.div(seq, NZ), lax.rem(seq, NZ)
    x_lo, y = lax.div(smp, NY), lax.rem(smp, NY)
    x = x_hi * 2 + x_lo

    def device(dx, dy, dz):
        xx, yy, zz = lax.rem(x + dx + NX, NX), lax.rem(y + dy + NY, NY), lax.rem(z + dz + NZ, NZ)
        return (grp, lax.rem(xx, 2) * NY + yy, lax.div(xx, 2) * NZ + zz)

    def rblock(lane, dz):
        column = x_hi if lane == 0 else 1 - x_hi
        return NPB + column * NZ + lax.rem(z + dz + NZ, NZ)

    def pblock(dx, dy):
        return lax.rem(x + dx + NX, NX) * NY + lax.rem(y + dy + NY, NY)

    peers = [device(0, 0, d) for d in range(1, NZ)]
    peers += [device(d, 0, 0) for d in range(1, NX)] + [device(0, 1, 0), device(0, -1, 0)]
    barrier = pltpu.get_barrier_semaphore()
    for peer in peers:
        pl.semaphore_signal(barrier, inc=1, device_id=peer, device_id_type=MESH)

    own_block, own_prompt = rblock(0, 0), pblock(0, 0)
    pairs = [(piece_in.at[:, k * HD : (k + 1) * HD], kv.at[k, own_prompt, 0:PIECE, :]) for k in range(PARTS)]
    pairs += [(own_in.at[:, k * HD : (k + 1) * HD], kv.at[k, own_block]) for k in range(PARTS)]
    pairs += [(q_in, q_ref), (len_in, len_ref), (order_in, order_ref), (tags_in, tags_ref), (weight_in, weight_ref)]
    loads = [pltpu.make_async_copy(src, dst, load_sem.at[i]) for i, (src, dst) in enumerate(pairs)]
    for load in loads:
        load.start()

    sent = {}
    numbers = {}

    def number(name):
        return numbers.setdefault(name, len(numbers))

    def piece_of(which, block, rows):
        start, size = rows
        return kv.at[which, block, pl.ds(start, size), :]

    def copy(name, ref, to):
        m = number(name)
        return pltpu.make_async_remote_copy(
            src_ref=ref[0], dst_ref=ref[1], send_sem=send_sem.at[m], recv_sem=recv_sem.at[m],
            device_id=to, device_id_type=MESH,
        )

    def send(name, which, block, rows, to, there=None):
        src = piece_of(which, block, rows)
        dst = src if there is None else piece_of(which, block, there)
        sent[name] = (which, rows)
        copy(name, (src, dst), to).start()

    def arrive(name, which, block, rows=ALL):
        here = piece_of(which, block, rows)
        copy(name, (here, here), device(0, 0, 1)).wait_recv()

    def z_step(kind, step):
        which, lane = KINDS[kind]
        low, high = (LOW, HIGH) if step == NZ // 2 else (ALL, ALL)
        send((kind, step, 1), which, rblock(lane, 1 - step), low, device(0, 0, 1))
        send((kind, step, -1), which, rblock(lane, step - 1), high, device(0, 0, -1))

    def z_arrive(kind, step):
        which, lane = KINDS[kind]
        low, high = (LOW, HIGH) if step == NZ // 2 else (ALL, ALL)
        arrive((kind, step, 1), which, rblock(lane, -step), low)
        arrive((kind, step, -1), which, rblock(lane, step), high)

    def x_step(step, rows, tag=0):
        low, high = (LOW, HIGH) if step == 2 else (rows, rows)
        send(("x", step, 1, tag), WHOLE, pblock(1 - step, 0), low, device(1, 0, 0))
        send(("x", step, -1, tag), WHOLE, pblock(step - 1, 0), high, device(-1, 0, 0))

    def x_arrive(step, rows, tag=0):
        low, high = (LOW, HIGH) if step == 2 else (rows, rows)
        arrive(("x", step, 1, tag), WHOLE, pblock(-step, 0), low)
        arrive(("x", step, -1, tag), WHOLE, pblock(step, 0), high)

    def y_step(dx, step, right=ALL, left=ALL, tag=0):
        send(("y", dx, step, 1, tag), WHOLE, pblock(dx, 1 - step), right, device(0, 1, 0))
        send(("y", dx, step, -1, tag), WHOLE, pblock(dx, step - 1), left, device(0, -1, 0))

    def y_arrive(dx, step, right=ALL, left=ALL, tag=0):
        arrive(("y", dx, step, 1, tag), WHOLE, pblock(dx, -step), right)
        arrive(("y", dx, step, -1, tag), WHOLE, pblock(dx, step), left)

    def far_step():
        for d in (1, -1):
            send(("far", d), WHOLE, pblock(0, 2), ALL, device(d, 0, 0))

    def far_arrive():
        for d in (1, -1):
            arrive(("far", d), WHOLE, pblock(-d, 2))

    def cross(step):
        for d in sorted({-step, step} if step < NZ // 2 else {step}):
            send(("cross", d), FEW, rblock(0, d), ALL, device(2, 0, 0))

    def cross_arrive(step):
        for d in sorted({-step, step} if step < NZ // 2 else {step}):
            arrive(("cross", d), FEW, rblock(1, d))

    for load in loads:
        load.wait()
    bias[0] = jnp.zeros((ROWS, ROWS), F32)

    def set_bias(block, _):
        bias[block + 1] = block_bias(order_ref, len_ref, seq, block)
        return 0

    lax.fori_loop(0, 2 * NZ, set_bias, 0)
    acc[...] = jnp.zeros_like(acc)

    pl.semaphore_wait(barrier, len(peers))

    slots = {0: 0, -1: 1, 1: 2, -2: 3, 2: 4, -3: 5, 3: 6, 4: 7}

    def slot(d):
        return (slots[d] * PIECE, PIECE)

    for d in (1, -1, 2, -2, 3, -3, 4):
        send(("piece", d), WHOLE, own_prompt, slot(0), device(0, 0, d), there=slot(-d if d < 4 else 4))
    send("most", MOST_OF, own_block, ALL, device(2, 0, 0))
    z_step("few", 1)
    z_step("own", 1)

    for h in range(KVH):
        for g in range(GW):
            column = (h * GW + g) * HD
            scaled = q_ref[:, column : column + HD].T.astype(F32) * SCALE
            high = scaled.astype(BF16)
            qa[h, 0:HD, g * ROWS : (g + 1) * ROWS] = high
            qa[h, HD : 2 * HD, g * ROWS : (g + 1) * ROWS] = (scaled - high.astype(F32)).astype(BF16)
    def pieces_arrive(distances):
        for d in distances:
            arrive(("piece", d), WHOLE, own_prompt, slot(-d if d < 4 else 4))

    def event_0():
        pieces_arrive((1, -1, 2, -2))
        y_step(0, 1, NEAR, NEAR)
        x_step(1, NEAR)
        z_arrive("few", 1)
        z_step("few", 2)
        arrive("most", MOST_OF, rblock(1, 0))
        z_step("other", 1)
        pieces_arrive((3, -3, 4))
        y_step(0, 1, FAR, FAR, 1)
        x_step(1, FAR, 1)
        cross(1)
        cross(0)

    def event_1():
        x_arrive(1, NEAR)
        y_step(1, 1, NEAR, NEAR)
        y_step(-1, 1, NEAR, NEAR)
        z_arrive("own", 1)
        z_step("own", 2)

    def event_2():
        y_arrive(0, 1, NEAR, NEAR)
        y_arrive(0, 1, FAR, FAR, 1)
        y_step(0, 2, LOW, HIGH)

    def event_3():
        z_arrive("few", 2)
        z_step("few", 3)
        cross(2)
        x_arrive(1, FAR, 1)
        x_step(2, ALL)
        y_step(1, 1, FAR, FAR, 1)
        y_step(-1, 1, FAR, FAR, 1)

    def event_4():
        z_arrive("other", 1)
        z_step("other", 2)
        z_arrive("own", 2)
        z_step("own", 3)

    def event_5():
        cross_arrive(1)

    def event_6():
        z_arrive("few", 3)
        z_step("few", 4)
        cross(3)
        y_arrive(0, 2, LOW, HIGH)
        far_step()
        cross_arrive(0)

    def event_7():
        x_arrive(2, ALL)
        y_step(2, 1, LOW, HIGH)
        y_step(2, 1, HIGH, LOW, 1)
        y_arrive(-1, 1, NEAR, NEAR)
        y_arrive(-1, 1, FAR, FAR, 1)

    def event_8():
        z_arrive("other", 2)
        z_step("other", 3)
        cross_arrive(2)

    def event_9():
        y_arrive(1, 1, NEAR, NEAR)
        y_arrive(1, 1, FAR, FAR, 1)

    def event_10():
        z_arrive("own", 3)
        z_step("own", 4)

    def event_11():
        z_arrive("few", 4)
        cross(4)
        y_arrive(2, 1, LOW, HIGH)
        y_step(2, 2, LOW, HIGH)
        y_arrive(2, 1, HIGH, LOW, 1)

    def event_12():
        z_arrive("other", 3)
        z_step("other", 4)
        cross_arrive(3)

    def event_13():
        far_arrive()

    def event_14():
        y_arrive(2, 2, LOW, HIGH)

    def event_15():
        z_arrive("own", 4)
        z_arrive("other", 4)
        cross_arrive(4)

    units = [
        (event_0, own_block, own_prompt),
        (event_1, rblock(0, -1), rblock(0, 1)),
        (event_2, pblock(0, -1), pblock(0, 1)),
        (event_3, pblock(1, 0), pblock(-1, 0)),
        (event_4, rblock(0, -2), rblock(0, 2)),
        (event_5, rblock(1, -1), rblock(1, 1)),
        (event_6, rblock(1, 0), pblock(0, 2)),
        (event_7, pblock(-1, -1), pblock(-1, 1)),
        (event_8, rblock(1, -2), rblock(1, 2)),
        (event_9, pblock(1, -1), pblock(1, 1)),
        (event_10, rblock(0, -3), rblock(0, 3)),
        (event_11, pblock(2, -1), pblock(2, 1)),
        (event_12, rblock(1, -3), rblock(1, 3)),
        (event_13, pblock(1, 2), pblock(-1, 2)),
        (event_14, pblock(2, 0), pblock(2, 2)),
        (event_15, rblock(0, 4), rblock(1, 4)),
    ]
    ones = jnp.ones((16, 2 * ROWS), BF16)

    def keep(unit, block, which):
        return pltpu.make_async_copy(kv.at[:, block], kept_ref.at[:, block], keep_sem.at[2 * unit + which])

    def pick(t, which):
        block = units[0][which]
        for i, unit in enumerate(units):
            block = jnp.where(t == i, unit[which], block)
        return block

    def work(t, one, two, finish=None):
        keep(t, one, 0).start()
        keep(t, two, 1).start()
        bias_one = bias.at[jnp.maximum(one - (NPB - 1), 0)]
        bias_two = bias.at[jnp.maximum(two - (NPB - 1), 0)]

        def scores(h):
            k = jnp.concatenate([kv[h, one], kv[h, two]], axis=0)
            return jnp.dot(jnp.concatenate([k, k], axis=1), qa[h], preferred_element_type=F32)

        def weights(s):
            b = jnp.concatenate([bias_one[...], bias_two[...]], axis=0)
            s = jnp.concatenate([s[:, g * ROWS : (g + 1) * ROWS] + b for g in range(GW)], axis=1)
            return jnp.exp2(s).astype(BF16)

        def mix(h, p):
            v = jnp.concatenate([kv[KVH + h, one].T, kv[KVH + h, two].T], axis=1)
            acc[h] += jnp.dot(jnp.concatenate([v, ones], axis=0), p, preferred_element_type=F32)

        s, p = {0: scores(0)}, {}
        for h in range(KVH + 1):
            if h + 1 < KVH:
                s[h + 1] = scores(h + 1)
            if h >= 1:
                mix(h - 1, p.pop(h - 1))
                if finish is not None:
                    finish(h - 1)
            if h < KVH:
                p[h] = weights(s.pop(h))

    def step(t, _):
        for i, unit in enumerate(units[:-1]):
            pl.when(t == i)(unit[0])
        work(t, pick(t, 1), pick(t, 2))
        return 0

    lax.fori_loop(0, len(units) - 1, step, 0)

    scale_row = row_scale(order_ref, len_ref, tags_ref, weight_ref, seq)
    spans = [slice(h * GW * HD, (h + 1) * GW * HD) for h in range(KVH)]
    stores = [pltpu.make_async_copy(out_ref.at[:, c], out_hbm.at[:, c], load_sem.at[i]) for i, c in enumerate(spans)]
    bad_ref[...] = jnp.zeros((1, ROWS), F32)

    def finish(h):
        bad = bad_ref[...]
        for g in range(GW):
            columns = slice(g * ROWS, (g + 1) * ROWS)
            total = acc[h, HD : HD + 1, columns]
            bad = jnp.where((total >= LEAST) & (total <= MOST), bad, 1.0)
            mixed = (acc[h, 0:HD, columns] * (scale_row / total)).astype(BF16)
            column = (h * GW + g) * HD
            out_ref[:, column : column + HD] = mixed.T
        bad_ref[...] = bad
        stores[h].start()

    last = len(units) - 1
    units[last][0]()
    work(last, units[last][1], units[last][2], finish)

    for store in stores:
        store.wait()
    for t, unit in enumerate(units):
        keep(t, unit[1], 0).wait()
        keep(t, unit[2], 1).wait()
    for name, (which, rows) in sent.items():
        here = piece_of(which, own_block, rows)
        copy(name, (here, here), device(0, 0, 1)).wait_send()


def check_rows(
    len_in, order_in, tags_in, weight_in, bad_in, q_ref, kept_ref, first_ref,
    out_ref,
    len_ref, order_ref, tags_ref, weight_ref, bad_ref, q, kv, out, sem, pass_sem,
):
    seq = lax.axis_index("seq")
    parts = [slice(i * ROWS // N_PASS, (i + 1) * ROWS // N_PASS) for i in range(N_PASS)]
    into = [pltpu.make_async_copy(first_ref.at[p], out.at[p], pass_sem.at[0, i]) for i, p in enumerate(parts)]
    onto = [pltpu.make_async_copy(out.at[p], out_ref.at[p], pass_sem.at[1, i]) for i, p in enumerate(parts)]
    flag = pltpu.make_async_copy(bad_in, bad_ref, sem)
    for load in into:
        load.start()
    flag.start()
    for load, store in zip(into, onto):
        load.wait()
        store.start()
    flag.wait()
    bad = jnp.max(bad_ref[...])
    for store in onto:
        store.wait()

    @pl.when(bad > 0.0)
    def redo():
        scalars = ((len_in, len_ref), (order_in, order_ref), (tags_in, tags_ref), (weight_in, weight_ref))
        for src, dst in ((q_ref, q), (kept_ref, kv), *scalars):
            fetch = pltpu.make_async_copy(src, dst, sem)
            fetch.start()
            fetch.wait()
        scale_row = row_scale(order_ref, len_ref, tags_ref, weight_ref, seq)

        def head(index, _):
            columns = pl.ds(pl.multiple_of(index * HD, HD), HD)
            kv_head = lax.div(index, GW)
            queries = q[:, columns]

            def scores(block):
                s = lax.dot_general(
                    kv[kv_head, block], queries, (((1,), (1,)), ((), ())), preferred_element_type=F32
                )
                b = block_bias(order_ref, len_ref, seq, jnp.maximum(block - NPB, 0))
                return jnp.where(block < NPB, s * SCALE, s * SCALE + b)

            def top_of(block, top):
                return jnp.maximum(top, jnp.max(scores(block), axis=0, keepdims=True))

            blocks = kv.shape[1]
            top = lax.fori_loop(0, blocks, top_of, jnp.full((1, ROWS), -jnp.inf, F32))

            def add(block, carry):
                total, mixed = carry
                w = jnp.exp2(scores(block) - top)
                total += jnp.sum(w, axis=0, keepdims=True)
                mixed += jnp.dot(kv[KVH + kv_head, block].T, w.astype(BF16), preferred_element_type=F32)
                return total, mixed

            total, mixed = lax.fori_loop(
                0, blocks, add, (jnp.zeros((1, ROWS), F32), jnp.zeros((HD, ROWS), F32))
            )
            out[:, columns] = (mixed * (scale_row / total)).astype(BF16).T
            return 0

        lax.fori_loop(0, H, head, 0)
        store = pltpu.make_async_copy(out, out_ref, sem)
        store.start()
        store.wait()


def shards(resp_q, resp_kv, prompt_kv, resp_len, block_order, tags, ver_weight):
    blocks = NPB + 2 * NZ
    vmem = pl.BlockSpec(memory_space=pltpu.VMEM)
    hbm = pl.BlockSpec(memory_space=pltpu.HBM)
    scalars = (resp_len, block_order, tags, ver_weight)
    queries = resp_q[0]
    kv_shape = (PARTS, blocks, ROWS, HD)
    keys = blocks * ROWS
    attended, bad, kept = pl.pallas_call(
        gather_attend,
        out_shape=(
            jax.ShapeDtypeStruct((ROWS, H * HD), BF16),
            jax.ShapeDtypeStruct((1, ROWS), F32),
            jax.ShapeDtypeStruct(kv_shape, BF16),
        ),
        in_specs=[hbm] * 7,
        out_specs=(hbm, vmem, hbm),
        scratch_shapes=[pltpu.SMEM(a.shape, a.dtype) for a in scalars]
        + [
            pltpu.VMEM((ROWS, H * HD), BF16),
            pltpu.VMEM((ROWS, H * HD), BF16),
            pltpu.VMEM(kv_shape, BF16),
            pltpu.VMEM((KVH, 2 * HD, GW * ROWS), BF16),
            pltpu.VMEM((KVH, HD + 16, GW * ROWS), F32),
            pltpu.VMEM((2 * NZ + 1, ROWS, ROWS), F32),
            pltpu.SemaphoreType.DMA((2 * PARTS + 5,)),
            pltpu.SemaphoreType.DMA((N_MSG,)),
            pltpu.SemaphoreType.DMA((N_MSG,)),
            pltpu.SemaphoreType.DMA((blocks,)),
        ],
        compiler_params=pltpu.CompilerParams(
            collective_id=0, has_side_effects=True, vmem_limit_bytes=60 * 2**20
        ),
        cost_estimate=pl.CostEstimate(
            flops=4 * ROWS * H * HD * keys, bytes_accessed=4 * keys * HALF, transcendentals=ROWS * H * keys
        ),
    )(*scalars, queries, resp_kv[0], prompt_kv)
    final = pl.pallas_call(
        check_rows,
        out_shape=jax.ShapeDtypeStruct((ROWS, H * HD), BF16),
        in_specs=[hbm] * 8,
        out_specs=hbm,
        scratch_shapes=[pltpu.SMEM(a.shape, a.dtype) for a in scalars]
        + [
            pltpu.VMEM((1, ROWS), F32),
            pltpu.VMEM((ROWS, H * HD), BF16),
            pltpu.VMEM(kv_shape, BF16),
            pltpu.VMEM((ROWS, H * HD), BF16),
            pltpu.SemaphoreType.DMA,
            pltpu.SemaphoreType.DMA((2, N_PASS)),
        ],
        compiler_params=pltpu.CompilerParams(vmem_limit_bytes=60 * 2**20),
    )(*scalars, bad, queries, kept, attended)
    return final[None]


def solution(mesh):
    in_specs = (
        P(("grp", "smp"), "seq", None),
        P(("grp", "smp"), "seq", None),
        P(("grp", "smp", "seq"), None),
        P(("grp", "smp")),
        P("grp"),
        P(("grp", "smp"), "seq"),
        P(),
    )
    out_specs = P(("grp", "smp"), "seq", None)
    return jax.shard_map(shards, mesh=mesh, in_specs=in_specs, out_specs=out_specs, check_vma=False)
```
